128 devices in a mesh: role: 2 (over core), dev: 64 (over z, x, y).
Axes of the slice: x: 4, y: 4, z: 4, core: 2. Of those that a mesh axis runs over, the one named last changes fastest.
Arguments:
- residual_in: bfloat16 [2048, 4096], P(('role', 'dev')), may hold values from -6 to 6
- queries: bfloat16 [2048, 8192], P(('role', 'dev')), may hold values from -6 to 6
- key_cache: bfloat16 [2048, 4, 128, 128], P(('role', 'dev')), may hold values from -6 to 6
- value_cache: bfloat16 [2048, 4, 128, 128], P(('role', 'dev')), may hold values from -6 to 6
- lengths: int32 [2048], P(('role', 'dev')), may hold values from 2 to 128, as said below
- out_weight: bfloat16 [8192, 4096], P('dev'), may hold values from -0.0625 to 0.0625
- norm_gain: float32 [4096], replicated, may hold values from 0.5 to 1.5
- expert_ids: int32 [2048, 8], P(('role', 'dev')), may hold values from 0 to 127, all different within a row; in each aligned block of 16 rows (0 to 15, 16 to 31, ...) at most 2 rows name the same one
- gate_values: float32 [2048, 8], P(('role', 'dev')), may hold values from 0.05 to 1
- w_gate: bfloat16 [128, 4096, 768], P(('role', 'dev')), may hold values from -0.09375 to 0.09375
- w_up: bfloat16 [128, 4096, 768], P(('role', 'dev')), may hold values from -0.09375 to 0.09375
- w_down: bfloat16 [128, 768, 4096], P(('role', 'dev')), may hold values from -0.21875 to 0.21875
Outputs:
- layer_out: bfloat16 [2048, 4096], P(('role', 'dev'))
The draws below stay inside these ranges and needn't reach their ends.
Inputs may be any that keep to these rules, and one draw needn't show every extreme that they name: `lengths`: every row has two or more live positions; some row has all 128 positions live. `expert_ids`: within the 16 rows of one device, no expert is chosen more than 2 times, a bound that some block reaches.
All inputs are finite; a program needn't handle non-finite values.
Results may differ from the reference program's by a relative error of at most 0.009.
Values may be sent and summed in bfloat16 or wider, within the bound.
No kernel may reach another device: no remote copies, remote signals or barrier semaphores. Data moves between devices by JAX's collectives and lax.ppermute only.
A program may use at most 128 MiB of HBM per device.

```python
import math
import jax
import jax.numpy as jnp
import numpy as np
from jax import lax

D = 4096
HQ = 64
KVH = 4
HD = 128
TOPK = 8
FFW = 768
L = 128
ROWS_DEV = 16
ROWS = 2048
EXPERTS = 128
CAP = 2


def draw_queries(key, part):
    key = jax.random.fold_in(key, 3)
    groups = HQ // KVH
    values = jnp.clip(jax.random.normal(key, (ROWS, KVH, groups, HD), jnp.float32), -6.0, 6.0)
    return values.reshape(ROWS, HQ * HD).astype(jnp.bfloat16)


def draw_key_cache(key, part):
    key = jax.random.fold_in(key, 7)
    values = jnp.clip(jax.random.normal(key, (ROWS, KVH, L, HD), jnp.float32), -6.0, 6.0)
    return values.astype(jnp.bfloat16)


def draw_lengths(key, part):
    key = jax.random.fold_in(key, 5)
    first, second = jax.random.split(key)
    values = jax.random.randint(first, (ROWS,), 2, L + 1)
    longest = jax.random.randint(second, (), 0, ROWS)
    return values.at[longest].set(L).astype(jnp.int32)


def level_of(key, shape, pieces, smallest, largest):
    loudness, own = 1.0, jax.random.fold_in(key, 6)
    for dim, shards_of in pieces:
        steps = jnp.exp(jax.random.uniform(jax.random.fold_in(own, dim), (shards_of,), jnp.float32, smallest / len(pieces), largest / len(pieces)))
        loudness = loudness * jnp.repeat(steps, shape[dim] // shards_of).reshape([-1 if axis == dim else 1 for axis in range(len(shape))])
    return loudness


def deal_out(rng, own, number, rows, number_of, top, bound, slope):
    sequence = jax.random.permutation(rng, number_of)
    packed, usual = shares(number_of, rows * top, bound, slope, True), shares(number_of, rows * top, bound, slope, False)
    places = jnp.arange(number_of)

    def named(sizes, offset_by):
        used = int((sizes > 0).sum())
        fixed = max(1, used // 4)
        passed = fixed + (places - fixed + offset_by * (used - fixed)) % max(1, number_of - fixed)
        return jnp.zeros((number_of,), jnp.int32).at[sequence[jnp.where(places < fixed, places, passed)]].set(jnp.asarray(sizes, jnp.int32))

    sizes = jnp.where(number % 4 == 0, named(packed, number // 4), named(usual, number - number // 4 - 1))
    mixed = jax.random.permutation(jax.random.fold_in(own, 3), number_of)
    donor, taker = mixed[0:number_of // 2 * 2:2], mixed[1:number_of // 2 * 2:2]
    margin = jnp.minimum(sizes[donor] - 1, bound - sizes[taker]) // 2
    margin = jnp.where((donor == sequence[0]) | (taker == sequence[0]) | (sizes[taker] == 0), 0, jnp.maximum(margin, 0))
    passed = jax.random.randint(jax.random.fold_in(own, 4), (number_of // 2,), 0, 1 << 20) % (margin + 1)
    sizes = sizes.at[donor].add(-passed).at[taker].add(passed)
    members = jnp.searchsorted(jnp.cumsum(sizes), jnp.arange(rows * top), side="right").astype(jnp.int32)
    table = members.reshape(top, rows).T
    table = table[jax.random.permutation(jax.random.fold_in(own, 1), rows)]
    offset_by = jax.random.randint(jax.random.fold_in(own, 2), (rows, 1), 0, top)
    return jnp.take_along_axis(table, (jnp.arange(top)[None, :] + offset_by) % top, axis=1)


def shares(count, total, limit, slope, full):
    weights = [(1 << 20) // math.isqrt(standing ** slope) + 1 for standing in range(1, count + 1)]
    largest = limit if full else min(limit, max(-(-total // count), total * weights[0] // sum(weights)))
    least = 1 if total - largest >= count - 1 else 0
    given, rest = [largest] + [least] * (count - 1), total - largest - least * (count - 1)
    while rest > 0:
        movable = [i for i in range(1, count) if given[i] < largest] or [i for i in range(1, count) if given[i] < limit]
        pool, remaining = sum([weights[i] for i in movable]), rest
        for i in movable:
            extra = min(limit - given[i], max(1, remaining * weights[i] // pool), rest)
            given[i] = given[i] + extra
            rest = rest - extra
    return np.array(given)


def scatter_about(key, extent, deviation, most, cuts=(), kind=jnp.bfloat16):
    entries = deviation * jax.random.normal(key, extent, jnp.float32)
    if cuts:
        entries = entries * level_of(key, extent, cuts, -0.22, 0.18)
    return jnp.clip(entries, -most, most).astype(kind)


def setup_inputs(seed: int = 0) -> dict:
    arg_keys = jax.random.split(jax.random.key(seed), 13)
    residual_in = scatter_about(arg_keys[0], (ROWS, D), 1.0, 6.0, ((0, 128),))
    queries = draw_queries(jax.random.fold_in(arg_keys[12], 71), 0)
    key_cache = draw_key_cache(jax.random.fold_in(arg_keys[12], 71), 0)
    value_cache = scatter_about(arg_keys[3], (ROWS, KVH, L, HD), 1.0, 6.0, ((0, 128),))
    lengths = draw_lengths(jax.random.fold_in(arg_keys[12], 71), 0)
    out_weight = scatter_about(arg_keys[5], (HQ * HD, D), (HQ * HD) ** -0.5, 0.0625, ((0, 64),))
    norm_gain = jnp.clip(1.0 + 0.1 * jax.random.normal(arg_keys[6], (D,), jnp.float32), 0.5, 1.5)
    expert_ids_keys = jax.random.split(jax.random.fold_in(arg_keys[7], 1), ROWS // ROWS_DEV)
    expert_ids_turns = jax.random.permutation(jax.random.fold_in(arg_keys[7], 3), ROWS // ROWS_DEV)
    expert_ids = jax.vmap(lambda own, number: deal_out(jax.random.fold_in(arg_keys[7], 2), own, number, ROWS_DEV, EXPERTS, TOPK, CAP, 2))(expert_ids_keys, expert_ids_turns).reshape((ROWS, TOPK))
    gate_values = jnp.clip(jnp.exp(math.log(1.0) - 2.9957323 * jax.random.uniform(arg_keys[8], (ROWS, TOPK), jnp.float32) ** level_of(arg_keys[8], (ROWS, TOPK), ((0, 128),), -0.2, 0.2)), 0.05, 1.0)
    w_gate = scatter_about(arg_keys[9], (EXPERTS, D, FFW), D ** -0.5, 0.09375, ((0, 128),))
    w_up = scatter_about(arg_keys[10], (EXPERTS, D, FFW), D ** -0.5, 0.09375, ((0, 128),))
    w_down = scatter_about(arg_keys[11], (EXPERTS, FFW, D), FFW ** -0.5, 0.21875, ((0, 128),))
    return {"residual_in": residual_in, "queries": queries, "key_cache": key_cache, "value_cache": value_cache, "lengths": lengths, "out_weight": out_weight, "norm_gain": norm_gain, "expert_ids": expert_ids, "gate_values": gate_values, "w_gate": w_gate, "w_up": w_up, "w_down": w_down}


def hadamard_table(order):
    indices = jnp.arange(order, dtype=jnp.int32)
    signs = jnp.ones((order, order), jnp.float32)
    stride = 1
    while stride < order:
        both = jnp.bitwise_and(jnp.bitwise_and(indices[:, None], stride), jnp.bitwise_and(indices[None, :], stride))
        signs = signs * jnp.where(both > 0, -1.0, 1.0).astype(jnp.float32)
        stride = stride * 2
    return signs / math.sqrt(order)

def run_expert(operands):
    rows, gate_mat, up_mat, down_mat = operands
    gate = jnp.dot(rows, gate_mat, preferred_element_type=jnp.float32)
    upper = jnp.dot(rows, up_mat, preferred_element_type=jnp.float32)
    act = (jax.nn.silu(gate) * upper).astype(jnp.bfloat16)
    return jnp.dot(act, down_mat, preferred_element_type=jnp.float32).astype(jnp.bfloat16)

def reference(residual_in, queries, key_cache, value_cache, lengths, out_weight, norm_gain, expert_ids, gate_values, w_gate, w_up, w_down):
    groups = HQ // KVH
    query_heads = queries.reshape(ROWS, KVH, groups, HD).astype(jnp.float32)
    scores = jnp.einsum('rkgd,rkld->rkgl', query_heads, key_cache.astype(jnp.float32)) / math.sqrt(HD)
    positions = jnp.arange(L, dtype=jnp.int32)
    live = positions[None, :] < lengths[:, None]
    scores = jnp.where(live[:, None, None, :], scores, -1e+30)
    peak = lax.optimization_barrier(jnp.max(scores, axis=-1, keepdims=True))
    weights = jnp.exp(scores - peak)
    probs = (weights / lax.optimization_barrier(jnp.sum(weights, axis=-1, keepdims=True))).astype(jnp.bfloat16)
    rotated = jnp.einsum('rkgl,rkld->rkgd', probs.astype(jnp.float32), value_cache.astype(jnp.float32)).astype(jnp.bfloat16)
    table = hadamard_table(HD)
    context = jnp.einsum('rkgd,de->rkge', rotated.astype(jnp.float32), table, precision=lax.Precision.HIGHEST).astype(jnp.bfloat16)
    attn = jnp.dot(context.reshape(ROWS, HQ * HD), out_weight, preferred_element_type=jnp.float32)
    hidden_state = residual_in.astype(jnp.float32) + attn
    scale = lax.rsqrt(lax.optimization_barrier(jnp.mean(hidden_state * hidden_state, axis=-1, keepdims=True)) + 1e-06)
    normed = (hidden_state * scale * norm_gain[None, :]).astype(jnp.bfloat16)
    mix = gate_values / lax.optimization_barrier(jnp.sum(gate_values, axis=-1, keepdims=True))
    blocks = ROWS // ROWS_DEV
    pairs = ROWS_DEV * TOPK
    flat = expert_ids.reshape(blocks, pairs).astype(jnp.int32)
    onehot = (flat[:, :, None] == jnp.arange(EXPERTS, dtype=jnp.int32)[None, None, :]).astype(jnp.int32)
    earlier = jnp.cumsum(onehot, axis=1) - onehot
    slots = lax.optimization_barrier(jnp.sum(earlier * onehot, axis=-1)).astype(jnp.int32)
    position = (jnp.arange(blocks, dtype=jnp.int32)[:, None] * CAP + slots).astype(jnp.int32)
    rows_of = jnp.broadcast_to(normed.reshape(ROWS, 1, D), (ROWS, TOPK, D)).reshape(ROWS * TOPK, D)
    expert_flat = flat.reshape(-1)
    position_flat = position.reshape(-1)
    buffer = jnp.zeros((EXPERTS, blocks * CAP, D), jnp.bfloat16).at[expert_flat, position_flat].set(rows_of)
    outputs = lax.map(run_expert, (buffer, w_gate, w_up, w_down))
    picked = outputs[expert_flat, position_flat].reshape(ROWS, TOPK, D).astype(jnp.float32)
    mixed = hidden_state + lax.optimization_barrier(jnp.sum(mix[:, :, None] * picked, axis=1))
    return mixed.astype(jnp.bfloat16)
```

```python
import functools
import math

import jax
import jax.numpy as jnp
from jax import lax
from jax.experimental import pallas as pl
from jax.experimental.pallas import tpu as pltpu
from jax.sharding import PartitionSpec as P

BF16 = jnp.bfloat16
F32 = jnp.float32


def sign_table(order):
    indices = jnp.arange(order, dtype=jnp.int32)
    signs = jnp.ones((order, order), F32)
    stride = 1
    while stride < order:
        both = (indices[:, None] & stride) & (indices[None, :] & stride)
        signs = signs * jnp.where(both > 0, -1.0, 1.0).astype(F32)
        stride = stride * 2
    return signs


def expert_kernel(pieces, slots, x_ref, gate_ref, up_ref, down_ref, out_ref, x_s, gate_s, up_s, act_s, res_s):
    step = pl.program_id(0)
    group = x_ref.shape[0] // pieces
    span = group // pieces
    row = lax.broadcasted_iota(jnp.int32, (group, group), 0)
    col = lax.broadcasted_iota(jnp.int32, (group, group), 1)

    @pl.when(step == 0)
    def _():
        spread = (col == (row % span) * pieces + row // span).astype(F32).astype(BF16)
        for g in range(pieces):
            y = jnp.dot(spread, x_ref[pl.ds(g * group, group), :], preferred_element_type=F32).astype(BF16)
            for j in range(pieces):
                x_s[j, pl.ds(g * span, span), :] = y[j * span:(j + 1) * span, :]
        gate_s[...] = jnp.zeros_like(gate_s)
        up_s[...] = jnp.zeros_like(up_s)

    @pl.when(step < pieces)
    def _():
        x = x_s[step]
        gate_s[...] += jnp.dot(x, gate_ref[...], preferred_element_type=F32)
        up_s[...] += jnp.dot(x, up_ref[...], preferred_element_type=F32)

    @pl.when(step == pieces)
    def _():
        gate = gate_s[...]
        act_s[...] = (gate / (1.0 + jnp.exp(-gate)) * up_s[...]).astype(BF16)

    @pl.when(step >= pieces)
    def _():
        j = step - pieces
        y = jnp.dot(act_s[...], down_ref[...], preferred_element_type=F32).astype(BF16)
        at = pl.multiple_of(j * span, span)
        for g in range(pieces):
            res_s[g, pl.ds(at, span), :] = y[g * span:(g + 1) * span, :]

    @pl.when(step == 2 * pieces - 1)
    def _():
        gather = (row == (col % span) * pieces + col // span).astype(F32).astype(BF16)
        for g in range(pieces):
            out_ref[pl.ds(g * group, group), :] = jnp.dot(
                gather, res_s[g], preferred_element_type=F32
            ).astype(BF16)


def experts(x, w_gate, w_up, w_down, pieces, slots):
    rows, block = x.shape
    width, hidden = w_gate.shape
    tokens = rows // pieces
    last = pieces - 1
    return pl.pallas_call(
        functools.partial(expert_kernel, pieces, slots),
        grid=(2 * pieces,),
        out_shape=jax.ShapeDtypeStruct((rows, block), BF16),
        in_specs=[
            pl.BlockSpec((rows, block), lambda i: (0, 0)),
            pl.BlockSpec((block, hidden), lambda i: (jnp.minimum(i, last), 0)),
            pl.BlockSpec((block, hidden), lambda i: (jnp.minimum(i, last), 0)),
            pl.BlockSpec((hidden, block), lambda i: (0, jnp.maximum(i - pieces, 0))),
        ],
        out_specs=pl.BlockSpec((rows, block), lambda i: (0, 0)),
        scratch_shapes=[
            pltpu.VMEM((pieces, tokens, block), BF16),
            pltpu.VMEM((tokens, hidden), F32),
            pltpu.VMEM((tokens, hidden), F32),
            pltpu.VMEM((tokens, hidden), BF16),
            pltpu.VMEM((pieces, rows // pieces, block), BF16),
        ],
        compiler_params=pltpu.CompilerParams(vmem_limit_bytes=40 * 1024 * 1024),
        cost_estimate=pl.CostEstimate(
            flops=6 * tokens * width * hidden,
            bytes_accessed=6 * width * hidden + 4 * rows * block,
            transcendentals=tokens * hidden,
        ),
    )(x, w_gate, w_up, w_down)


def shards(
    residual_in,
    queries,
    key_cache,
    value_cache,
    lengths,
    out_weight,
    norm_gain,
    expert_ids,
    gate_values,
    w_gate,
    w_up,
    w_down,
):
    rows = queries.shape[0]
    kv_heads, cache_len, head_dim = key_cache.shape[1:]
    head_total = queries.shape[1] // head_dim
    width = residual_in.shape[1]
    chips = lax.axis_size("dev")
    pieces = 8
    clusters = chips // pieces
    block = width // pieces

    teams = [[c * pieces + i for i in range(pieces)] for c in range(clusters)]
    weight = out_weight.reshape(out_weight.shape[0], pieces, block).transpose(1, 0, 2)
    weight = lax.all_to_all(weight, "dev", 0, 0, tiled=True, axis_index_groups=teams)
    weight = weight.reshape(pieces * out_weight.shape[0], block)

    query_heads = queries.reshape(rows, kv_heads, head_total // kv_heads, head_dim)
    scores = jnp.einsum(
        "rkgd,rkld->rkgl", query_heads, key_cache, preferred_element_type=F32
    ) / math.sqrt(head_dim)
    positions = jnp.arange(cache_len, dtype=jnp.int32)
    live = positions[None, :] < lengths[:, None]
    scores = jnp.where(live[:, None, None, :], scores, -1e30)
    peak = jnp.max(scores, axis=-1, keepdims=True)
    weights = jnp.exp(scores - peak)
    probs = (weights / jnp.sum(weights, axis=-1, keepdims=True)).astype(BF16)
    rotated = jnp.einsum(
        "rkgl,rkld->rkgd", probs, value_cache, preferred_element_type=F32
    ).astype(BF16)
    table = sign_table(head_dim).astype(BF16)
    context = jnp.dot(
        rotated.reshape(rows * head_total, head_dim), table, preferred_element_type=F32
    ) * (1.0 / math.sqrt(head_dim))
    context = context.astype(BF16).reshape(rows, clusters, pieces * head_dim).transpose(1, 0, 2)
    context = jnp.broadcast_to(
        context[:, None], (clusters, pieces, rows, pieces * head_dim)
    ).reshape(chips, rows, pieces * head_dim)
    context = lax.all_to_all(context, "dev", 0, 0, tiled=True)
    part = jnp.dot(
        context.reshape(chips * rows, pieces * head_dim), weight, preferred_element_type=F32
    ).astype(BF16)
    part = lax.all_to_all(part.reshape(chips, rows, block), "dev", 0, 0, tiled=True)
    attn = jnp.sum(part.reshape(clusters, pieces, rows, block).astype(F32), axis=0)

    residual = residual_in.reshape(rows, pieces, block).transpose(1, 0, 2)
    hidden = residual.astype(F32) + attn
    scale = lax.rsqrt(jnp.sum(hidden * hidden, axis=(0, 2), keepdims=True) / width + 1e-06)
    normed = (hidden * scale * norm_gain.reshape(pieces, 1, block)).astype(BF16)
    normed = normed.reshape(pieces * rows, block)

    top = expert_ids.shape[1]
    expert_total = chips * lax.axis_size("role")
    slots = 2
    pairs = rows * top
    flat = expert_ids.reshape(pairs)
    same = flat[:, None] == flat[None, :]
    before = jnp.arange(pairs)[:, None] > jnp.arange(pairs)[None, :]
    slot = jnp.sum((same & before).astype(jnp.int32), axis=1)
    target = (flat * slots + slot).reshape(rows, top)
    places = expert_total * slots * pieces
    spot = target[None] * pieces + jnp.arange(pieces, dtype=jnp.int32)[:, None, None]
    spot = spot.reshape(pieces * rows, top)
    chosen = jnp.zeros((places, pieces * rows), jnp.bool_)
    for k in range(top):
        chosen = chosen | (jnp.arange(places, dtype=jnp.int32)[:, None] == spot[:, k][None, :])
    outgoing = jnp.dot(chosen.astype(BF16), normed, preferred_element_type=F32).astype(BF16)
    arrived = lax.all_to_all(
        outgoing.reshape(expert_total, slots * pieces, block), ("role", "dev"), 0, 0, tiled=True
    )
    result = experts(
        arrived.reshape(places, block), w_gate[0], w_up[0], w_down[0], pieces, slots
    )
    replies = lax.all_to_all(
        result.reshape(expert_total, slots * pieces, block), ("role", "dev"), 0, 0, tiled=True
    )
    mix = gate_values / jnp.sum(gate_values, axis=-1, keepdims=True)
    mix = jnp.broadcast_to(mix[None], (pieces, rows, top)).reshape(pieces * rows, top)
    mixer = jnp.zeros((pieces * rows, places), F32)
    for k in range(top):
        here = jnp.arange(places, dtype=jnp.int32)[None, :] == spot[:, k][:, None]
        mixer = mixer + jnp.where(here, mix[:, k][:, None], 0.0)
    rounded = lax.reduce_precision(mixer, exponent_bits=8, mantissa_bits=7)
    high = rounded.astype(BF16)
    low = (mixer - rounded).astype(BF16)
    both = jnp.dot(
        jnp.concatenate([high, low], axis=0),
        replies.reshape(places, block),
        preferred_element_type=F32,
    )
    mixed = hidden + (both[: pieces * rows] + both[pieces * rows :]).reshape(pieces, rows, block)
    return mixed.astype(BF16).transpose(1, 0, 2).reshape(rows, width)


def solution(mesh):
    both = ("role", "dev")
    return jax.shard_map(
        shards,
        mesh=mesh,
        in_specs=(
            P(both, None),
            P(both, None),
            P(both, None, None, None),
            P(both, None, None, None),
            P(both),
            P("dev", None),
            P(),
            P(both, None),
            P(both, None),
            P(both, None, None),
            P(both, None, None),
            P(both, None, None),
        ),
        out_specs=P(both, None),
        check_vma=False,
    )
```

```python
import functools
import math

import jax
import jax.numpy as jnp
from jax import lax
from jax.experimental import pallas as pl
from jax.experimental.pallas import tpu as pltpu
from jax.sharding import PartitionSpec as P

BF16 = jnp.bfloat16
F32 = jnp.float32


def sign_table(order):
    indices = jnp.arange(order, dtype=jnp.int32)
    signs = jnp.ones((order, order), F32)
    stride = 1
    while stride < order:
        both = (indices[:, None] & stride) & (indices[None, :] & stride)
        signs = signs * jnp.where(both > 0, -1.0, 1.0).astype(F32)
        stride = stride * 2
    return signs


def expert_kernel(pieces, x_hbm, gate_hbm, up_hbm, down_hbm, out_hbm,
                  in_s, x_s, gate_s, up_s, down_s, act_s, res_s, out_s, x_sem, w_sem, d_sem, o_sem):
    group, block = in_s.shape[1:]
    span = group // pieces
    parts, _, wide = gate_s.shape
    outs, _, tall = down_s.shape
    loads = [pltpu.make_async_copy(x_hbm, in_s, x_sem)]
    for i in range(parts):
        cut = pl.ds(i * wide, wide)
        loads.append(pltpu.make_async_copy(gate_hbm.at[:, cut], gate_s.at[i], w_sem.at[i, 0]))
        loads.append(pltpu.make_async_copy(up_hbm.at[:, cut], up_s.at[i], w_sem.at[i, 1]))
    for i in range(outs):
        loads.append(pltpu.make_async_copy(down_hbm.at[:, pl.ds(i * tall, tall)], down_s.at[i], d_sem.at[i]))
    for load in loads:
        load.start()

    row = lax.broadcasted_iota(jnp.int32, (group, group), 0)
    col = lax.broadcasted_iota(jnp.int32, (group, group), 1)
    spread = (col == (row % span) * pieces + row // span).astype(F32).astype(BF16)
    gather = (row == (col % span) * pieces + col // span).astype(F32).astype(BF16)
    loads[0].wait()
    for g in range(in_s.shape[0]):
        y = jnp.dot(spread, in_s[g], preferred_element_type=F32).astype(BF16)
        for j in range(pieces):
            x_s[g * span:(g + 1) * span, j * block:(j + 1) * block] = y[j * span:(j + 1) * span, :]
    for i in range(parts):
        loads[1 + 2 * i].wait()
        gate = jnp.dot(x_s[...], gate_s[i], preferred_element_type=F32)
        loads[2 + 2 * i].wait()
        up = jnp.dot(x_s[...], up_s[i], preferred_element_type=F32)
        act_s[:, i * wide:(i + 1) * wide] = (gate / (1.0 + jnp.exp(-gate)) * up).astype(BF16)
    for i in range(outs):
        loads[1 + 2 * parts + i].wait()
        y = jnp.dot(act_s[...], down_s[i], preferred_element_type=F32).astype(BF16)
        for n in range(tall // block):
            j = i * (tall // block) + n
            for g in range(in_s.shape[0]):
                res_s[g, j * span:(j + 1) * span, :] = y[g * span:(g + 1) * span, n * block:(n + 1) * block]
    stores = []
    for g in range(in_s.shape[0]):
        out_s[g] = jnp.dot(gather, res_s[g], preferred_element_type=F32).astype(BF16)
        store = pltpu.make_async_copy(out_s.at[g], out_hbm.at[g], o_sem.at[g])
        store.start()
        stores.append(store)
    for store in stores:
        store.wait()


def experts(x, w_gate, w_up, w_down, pieces):
    rows, block = x.shape
    width, hidden = w_gate.shape
    tokens = rows // pieces
    groups = pieces
    group = rows // groups
    wide, tall = 256, 1024
    if hidden % wide or width % tall or tall % block:
        wide, tall = hidden, width
    parts, outs = hidden // wide, width // tall
    result = pl.pallas_call(
        functools.partial(expert_kernel, pieces),
        out_shape=jax.ShapeDtypeStruct((groups, group, block), BF16),
        in_specs=[pl.BlockSpec(memory_space=pl.ANY)] * 4,
        out_specs=pl.BlockSpec(memory_space=pl.ANY),
        scratch_shapes=[
            pltpu.VMEM((groups, group, block), BF16),
            pltpu.VMEM((tokens, width), BF16),
            pltpu.VMEM((parts, width, wide), BF16),
            pltpu.VMEM((parts, width, wide), BF16),
            pltpu.VMEM((outs, hidden, tall), BF16),
            pltpu.VMEM((tokens, hidden), BF16),
            pltpu.VMEM((groups, group, block), BF16),
            pltpu.VMEM((groups, group, block), BF16),
            pltpu.SemaphoreType.DMA,
            pltpu.SemaphoreType.DMA((parts, 2)),
            pltpu.SemaphoreType.DMA((outs,)),
            pltpu.SemaphoreType.DMA((groups,)),
        ],
        compiler_params=pltpu.CompilerParams(vmem_limit_bytes=52 * 1024 * 1024),
        cost_estimate=pl.CostEstimate(
            flops=6 * tokens * width * hidden,
            bytes_accessed=6 * width * hidden + 4 * rows * block,
            transcendentals=tokens * hidden,
        ),
    )(x.reshape(groups, group, block), w_gate, w_up, w_down)
    return result.reshape(rows, block)


def project_kernel(a_ref, w_ref, out_ref):
    out_ref[...] = jnp.dot(a_ref[...], w_ref[...], preferred_element_type=F32).astype(BF16)


def project(a, w):
    rows, depth = a.shape
    columns = w.shape[1]
    tile = 256
    return pl.pallas_call(
        project_kernel,
        grid=(rows // tile,),
        out_shape=jax.ShapeDtypeStruct((rows, columns), BF16),
        in_specs=[
            pl.BlockSpec((tile, depth), lambda i: (i, 0)),
            pl.BlockSpec((depth, columns), lambda i: (0, 0)),
        ],
        out_specs=pl.BlockSpec((tile, columns), lambda i: (i, 0)),
        compiler_params=pltpu.CompilerParams(vmem_limit_bytes=24 * 1024 * 1024),
        cost_estimate=pl.CostEstimate(
            flops=2 * rows * depth * columns,
            bytes_accessed=2 * (rows * depth + depth * columns + rows * columns),
            transcendentals=0,
        ),
    )(a, w)


def shards(
    residual_in,
    queries,
    key_cache,
    value_cache,
    lengths,
    out_weight,
    norm_gain,
    expert_ids,
    gate_values,
    w_gate,
    w_up,
    w_down,
):
    rows = queries.shape[0]
    kv_heads, cache_len, head_dim = key_cache.shape[1:]
    head_total = queries.shape[1] // head_dim
    width = residual_in.shape[1]
    chips = lax.axis_size("dev")
    pieces = 8
    clusters = chips // pieces
    block = width // pieces

    teams = [[c * pieces + i for i in range(pieces)] for c in range(clusters)]
    weight = out_weight.reshape(out_weight.shape[0], pieces, block).transpose(1, 0, 2)
    weight = lax.all_to_all(weight, "dev", 0, 0, tiled=True, axis_index_groups=teams)
    weight = weight.reshape(pieces * out_weight.shape[0], block)

    query_heads = queries.reshape(rows, kv_heads, head_total // kv_heads, head_dim)
    scores = jnp.einsum(
        "rkgd,rkld->rkgl", query_heads, key_cache, preferred_element_type=F32
    ) / math.sqrt(head_dim)
    positions = jnp.arange(cache_len, dtype=jnp.int32)
    live = positions[None, :] < lengths[:, None]
    scores = jnp.where(live[:, None, None, :], scores, -1e30)
    peak = jnp.max(scores, axis=-1, keepdims=True)
    weights = jnp.exp(scores - peak)
    probs = (weights / jnp.sum(weights, axis=-1, keepdims=True)).astype(BF16)
    rotated = jnp.einsum(
        "rkgl,rkld->rkgd", probs, value_cache, preferred_element_type=F32
    ).astype(BF16)
    table = sign_table(head_dim).astype(BF16)
    context = jnp.dot(
        rotated.reshape(rows * head_total, head_dim), table, preferred_element_type=F32
    ) * (1.0 / math.sqrt(head_dim))
    context = context.astype(BF16).reshape(rows, clusters, pieces * head_dim).transpose(1, 0, 2)
    context = jnp.broadcast_to(
        context[:, None], (clusters, pieces, rows, pieces * head_dim)
    ).reshape(chips, rows, pieces * head_dim)
    context = lax.all_to_all(context, "dev", 0, 0, tiled=True)
    part = project(context.reshape(chips * rows, pieces * head_dim), weight)
    part = lax.all_to_all(part.reshape(chips, rows, block), "dev", 0, 0, tiled=True)
    attn = jnp.sum(part.reshape(clusters, pieces, rows, block).astype(F32), axis=0)

    residual = residual_in.reshape(rows, pieces, block).transpose(1, 0, 2)
    hidden = residual.astype(F32) + attn
    scale = lax.rsqrt(jnp.sum(hidden * hidden, axis=(0, 2), keepdims=True) / width + 1e-06)
    normed = (hidden * scale * norm_gain.reshape(pieces, 1, block)).astype(BF16)
    normed = normed.reshape(pieces * rows, block)

    top = expert_ids.shape[1]
    expert_total = chips * lax.axis_size("role")
    slots = 2
    pairs = rows * top
    flat = expert_ids.reshape(pairs)
    same = flat[:, None] == flat[None, :]
    before = jnp.arange(pairs)[:, None] > jnp.arange(pairs)[None, :]
    slot = jnp.sum((same & before).astype(jnp.int32), axis=1)
    target = (flat * slots + slot).reshape(rows, top)
    places = expert_total * slots * pieces
    spot = target[None] * pieces + jnp.arange(pieces, dtype=jnp.int32)[:, None, None]
    spot = spot.reshape(pieces * rows, top)
    chosen = jnp.zeros((places, pieces * rows), jnp.bool_)
    for k in range(top):
        chosen = chosen | (jnp.arange(places, dtype=jnp.int32)[:, None] == spot[:, k][None, :])
    outgoing = jnp.dot(chosen.astype(BF16), normed, preferred_element_type=F32).astype(BF16)
    arrived = lax.all_to_all(
        outgoing.reshape(expert_total, slots * pieces, block), ("role", "dev"), 0, 0, tiled=True
    )
    result = experts(
        arrived.reshape(places, block), w_gate[0], w_up[0], w_down[0], pieces
    )
    replies = lax.all_to_all(
        result.reshape(expert_total, slots * pieces, block), ("role", "dev"), 0, 0, tiled=True
    )
    mix = gate_values / jnp.sum(gate_values, axis=-1, keepdims=True)
    mix = jnp.broadcast_to(mix[None], (pieces, rows, top)).reshape(pieces * rows, top)
    mixer = jnp.zeros((pieces * rows, places), F32)
    for k in range(top):
        here = jnp.arange(places, dtype=jnp.int32)[None, :] == spot[:, k][:, None]
        mixer = mixer + jnp.where(here, mix[:, k][:, None], 0.0)
    rounded = lax.reduce_precision(mixer, exponent_bits=8, mantissa_bits=7)
    high = rounded.astype(BF16)
    low = (mixer - rounded).astype(BF16)
    both = jnp.dot(
        jnp.concatenate([high, low], axis=0),
        replies.reshape(places, block),
        preferred_element_type=F32,
    )
    mixed = hidden + (both[: pieces * rows] + both[pieces * rows :]).reshape(pieces, rows, block)
    return mixed.astype(BF16).transpose(1, 0, 2).reshape(rows, width)


def solution(mesh):
    both = ("role", "dev")
    return jax.shard_map(
        shards,
        mesh=mesh,
        in_specs=(
            P(both, None),
            P(both, None),
            P(both, None, None, None),
            P(both, None, None, None),
            P(both),
            P("dev", None),
            P(),
            P(both, None),
            P(both, None),
            P(both, None, None),
            P(both, None, None),
            P(both, None, None),
        ),
        out_specs=P(both, None),
        check_vma=False,
    )
```

```python
import functools
import math

import jax
import jax.numpy as jnp
import numpy as np
from jax import lax
from jax.experimental import pallas as pl
from jax.experimental.pallas import tpu as pltpu
from jax.sharding import PartitionSpec as P

BF16 = jnp.bfloat16
F32 = jnp.float32


def sign_table(order):
    signs = np.ones((1, 1), np.float32)
    while signs.shape[0] < order:
        signs = np.block([[signs, signs], [signs, -signs]])
    return signs


def attend_kernel(copies, len_ref, q_ref, k_ref, v_ref, table_ref, out_ref):
    rows, _, cache_len, dim = k_ref.shape
    heads = q_ref.shape[1] // dim
    total = rows * heads
    at = lax.broadcasted_iota(jnp.int32, (total, total), 0)
    to = lax.broadcasted_iota(jnp.int32, (total, total), 1)
    turn_in = (to == (at % heads) * rows + at // heads).astype(F32).astype(BF16)
    turn_out = (to == (at % rows) * heads + at // rows).astype(F32).astype(BF16)
    stacked = jnp.concatenate([q_ref[:, h * dim:(h + 1) * dim] for h in range(heads)], axis=0)
    q = jnp.dot(turn_in, stacked, preferred_element_type=F32).astype(BF16)
    position = lax.broadcasted_iota(jnp.int32, (heads, cache_len), 1)
    scores = []
    for r in range(rows):
        s = lax.dot_general(
            q[r * heads:(r + 1) * heads], k_ref[r, 0], (((1,), (1,)), ((), ())), preferred_element_type=F32
        )
        scores.append(jnp.where(position < len_ref[r], s * (1.0 / math.sqrt(dim)), -1e30))
    scores = jnp.concatenate(scores, axis=0)
    weights = jnp.exp(scores - jnp.max(scores, axis=-1, keepdims=True))
    probs = (weights / jnp.sum(weights, axis=-1, keepdims=True)).astype(BF16)
    rotated = jnp.concatenate(
        [
            jnp.dot(probs[r * heads:(r + 1) * heads], v_ref[r, 0], preferred_element_type=F32).astype(BF16)
            for r in range(rows)
        ],
        axis=0,
    )
    turned = jnp.dot(turn_out, rotated, preferred_element_type=F32).astype(BF16)
    context = jnp.dot(turned, table_ref[...], preferred_element_type=F32) * (1.0 / math.sqrt(dim))
    context = context.astype(BF16)
    each = out_ref.shape[3] // dim
    for h in range(heads):
        piece = context[h * rows:(h + 1) * rows]
        for c in range(copies):
            out_ref[h // each, c, :, (h % each) * dim:(h % each + 1) * dim] = piece


def attend(lengths, queries, key_cache, value_cache, clusters, copies):
    rows, kv_heads, cache_len, dim = key_cache.shape
    share = queries.shape[1] // kv_heads
    columns = queries.shape[1] // clusters
    table = jnp.asarray(sign_table(dim), BF16)
    per = clusters // kv_heads
    return pl.pallas_call(
        functools.partial(attend_kernel, copies),
        grid=(kv_heads,),
        out_shape=jax.ShapeDtypeStruct((clusters, copies, rows, columns), BF16),
        in_specs=[
            pl.BlockSpec(memory_space=pltpu.SMEM),
            pl.BlockSpec((rows, share), lambda i: (0, i)),
            pl.BlockSpec((rows, 1, cache_len, dim), lambda i: (0, i, 0, 0)),
            pl.BlockSpec((rows, 1, cache_len, dim), lambda i: (0, i, 0, 0)),
            pl.BlockSpec((dim, dim), lambda i: (0, 0)),
        ],
        out_specs=pl.BlockSpec((per, copies, rows, columns), lambda i: (i, 0, 0, 0)),
        compiler_params=pltpu.CompilerParams(vmem_limit_bytes=24 * 1024 * 1024),
        cost_estimate=pl.CostEstimate(
            flops=4 * rows * queries.shape[1] * cache_len,
            bytes_accessed=4 * rows * kv_heads * cache_len * dim + 2 * clusters * copies * rows * columns,
            transcendentals=rows * queries.shape[1] // dim * cache_len,
        ),
    )(lengths, queries, key_cache, value_cache, table)


def expert_kernel(pieces, x_hbm, gate_hbm, up_hbm, down_hbm, out_hbm,
                  in_s, x_s, gate_s, up_s, down_s, act_s, res_s, out_s, x_sem, w_sem, d_sem, o_sem):
    group, block = in_s.shape[1:]
    span = group // pieces
    parts, _, wide = gate_s.shape
    outs, _, tall = down_s.shape
    loads = [pltpu.make_async_copy(x_hbm, in_s, x_sem)]
    for i in range(parts):
        cut = pl.ds(i * wide, wide)
        loads.append(pltpu.make_async_copy(gate_hbm.at[:, cut], gate_s.at[i], w_sem.at[i, 0]))
        loads.append(pltpu.make_async_copy(up_hbm.at[:, cut], up_s.at[i], w_sem.at[i, 1]))
    for i in range(outs):
        loads.append(pltpu.make_async_copy(down_hbm.at[:, pl.ds(i * tall, tall)], down_s.at[i], d_sem.at[i]))
    for load in loads:
        load.start()

    row = lax.broadcasted_iota(jnp.int32, (group, group), 0)
    col = lax.broadcasted_iota(jnp.int32, (group, group), 1)
    spread = (col == (row % span) * pieces + row // span).astype(F32).astype(BF16)
    gather = (row == (col % span) * pieces + col // span).astype(F32).astype(BF16)
    loads[0].wait()
    for g in range(in_s.shape[0]):
        y = jnp.dot(spread, in_s[g], preferred_element_type=F32).astype(BF16)
        for j in range(pieces):
            x_s[g * span:(g + 1) * span, j * block:(j + 1) * block] = y[j * span:(j + 1) * span, :]
    for i in range(parts):
        loads[1 + 2 * i].wait()
        gate = jnp.dot(x_s[...], gate_s[i], preferred_element_type=F32)
        loads[2 + 2 * i].wait()
        up = jnp.dot(x_s[...], up_s[i], preferred_element_type=F32)
        act_s[:, i * wide:(i + 1) * wide] = (gate / (1.0 + jnp.exp(-gate)) * up).astype(BF16)
    for i in range(outs):
        loads[1 + 2 * parts + i].wait()
        y = jnp.dot(act_s[...], down_s[i], preferred_element_type=F32).astype(BF16)
        for n in range(tall // block):
            j = i * (tall // block) + n
            for g in range(in_s.shape[0]):
                res_s[g, j * span:(j + 1) * span, :] = y[g * span:(g + 1) * span, n * block:(n + 1) * block]
    stores = []
    for g in range(in_s.shape[0]):
        out_s[g] = jnp.dot(gather, res_s[g], preferred_element_type=F32).astype(BF16)
        store = pltpu.make_async_copy(out_s.at[g], out_hbm.at[g], o_sem.at[g])
        store.start()
        stores.append(store)
    for store in stores:
        store.wait()


def experts(x, w_gate, w_up, w_down, pieces):
    rows, block = x.shape
    width, hidden = w_gate.shape
    tokens = rows // pieces
    groups = pieces
    group = rows // groups
    wide, tall = 256, 1024
    if hidden % wide or width % tall or tall % block:
        wide, tall = hidden, width
    parts, outs = hidden // wide, width // tall
    result = pl.pallas_call(
        functools.partial(expert_kernel, pieces),
        out_shape=jax.ShapeDtypeStruct((groups, group, block), BF16),
        in_specs=[pl.BlockSpec(memory_space=pl.ANY)] * 4,
        out_specs=pl.BlockSpec(memory_space=pl.ANY),
        scratch_shapes=[
            pltpu.VMEM((groups, group, block), BF16),
            pltpu.VMEM((tokens, width), BF16),
            pltpu.VMEM((parts, width, wide), BF16),
            pltpu.VMEM((parts, width, wide), BF16),
            pltpu.VMEM((outs, hidden, tall), BF16),
            pltpu.VMEM((tokens, hidden), BF16),
            pltpu.VMEM((groups, group, block), BF16),
            pltpu.VMEM((groups, group, block), BF16),
            pltpu.SemaphoreType.DMA,
            pltpu.SemaphoreType.DMA((parts, 2)),
            pltpu.SemaphoreType.DMA((outs,)),
            pltpu.SemaphoreType.DMA((groups,)),
        ],
        compiler_params=pltpu.CompilerParams(vmem_limit_bytes=52 * 1024 * 1024),
        cost_estimate=pl.CostEstimate(
            flops=6 * tokens * width * hidden,
            bytes_accessed=6 * width * hidden + 4 * rows * block,
            transcendentals=tokens * hidden,
        ),
    )(x.reshape(groups, group, block), w_gate, w_up, w_down)
    return result.reshape(rows, block)


def project_kernel(a_ref, w_ref, out_ref):
    out_ref[...] = jnp.dot(a_ref[...], w_ref[...], preferred_element_type=F32).astype(BF16)


def project(a, w):
    rows, depth = a.shape
    columns = w.shape[1]
    tile = 256
    return pl.pallas_call(
        project_kernel,
        grid=(rows // tile,),
        out_shape=jax.ShapeDtypeStruct((rows, columns), BF16),
        in_specs=[
            pl.BlockSpec((tile, depth), lambda i: (i, 0)),
            pl.BlockSpec((depth, columns), lambda i: (0, 0)),
        ],
        out_specs=pl.BlockSpec((tile, columns), lambda i: (i, 0)),
        compiler_params=pltpu.CompilerParams(vmem_limit_bytes=24 * 1024 * 1024),
        cost_estimate=pl.CostEstimate(
            flops=2 * rows * depth * columns,
            bytes_accessed=2 * (rows * depth + depth * columns + rows * columns),
            transcendentals=0,
        ),
    )(a, w)


def shards(
    residual_in,
    queries,
    key_cache,
    value_cache,
    lengths,
    out_weight,
    norm_gain,
    expert_ids,
    gate_values,
    w_gate,
    w_up,
    w_down,
):
    rows = queries.shape[0]
    head_dim = key_cache.shape[3]
    width = residual_in.shape[1]
    chips = lax.axis_size("dev")
    pieces = 8
    clusters = chips // pieces
    block = width // pieces

    teams = [[c * pieces + i for i in range(pieces)] for c in range(clusters)]
    weight = out_weight.reshape(out_weight.shape[0], pieces, block).transpose(1, 0, 2)
    weight = lax.all_to_all(weight, "dev", 0, 0, tiled=True, axis_index_groups=teams)
    weight = weight.reshape(pieces * out_weight.shape[0], block)

    context = attend(lengths, queries, key_cache, value_cache, clusters, pieces)
    context = context.reshape(chips, rows, pieces * head_dim)
    context = lax.all_to_all(context, "dev", 0, 0, tiled=True)
    part = project(context.reshape(chips * rows, pieces * head_dim), weight)
    part = lax.all_to_all(part.reshape(chips, rows, block), "dev", 0, 0, tiled=True)
    attn = jnp.sum(part.reshape(clusters, pieces, rows, block).astype(F32), axis=0)

    residual = residual_in.reshape(rows, pieces, block).transpose(1, 0, 2)
    hidden = residual.astype(F32) + attn
    scale = lax.rsqrt(jnp.sum(hidden * hidden, axis=(0, 2), keepdims=True) / width + 1e-06)
    normed = (hidden * scale * norm_gain.reshape(pieces, 1, block)).astype(BF16)
    normed = normed.reshape(pieces * rows, block)

    top = expert_ids.shape[1]
    expert_total = chips * lax.axis_size("role")
    slots = 2
    pairs = rows * top
    flat = expert_ids.reshape(pairs)
    same = flat[:, None] == flat[None, :]
    before = jnp.arange(pairs)[:, None] > jnp.arange(pairs)[None, :]
    slot = jnp.sum((same & before).astype(jnp.int32), axis=1)
    target = (flat * slots + slot).reshape(rows, top)
    places = expert_total * slots * pieces
    spot = target[None] * pieces + jnp.arange(pieces, dtype=jnp.int32)[:, None, None]
    spot = spot.reshape(pieces * rows, top)
    chosen = jnp.zeros((places, pieces * rows), jnp.bool_)
    for k in range(top):
        chosen = chosen | (jnp.arange(places, dtype=jnp.int32)[:, None] == spot[:, k][None, :])
    outgoing = jnp.dot(chosen.astype(BF16), normed, preferred_element_type=F32).astype(BF16)
    arrived = lax.all_to_all(
        outgoing.reshape(expert_total, slots * pieces, block), ("role", "dev"), 0, 0, tiled=True
    )
    result = experts(
        arrived.reshape(places, block), w_gate[0], w_up[0], w_down[0], pieces
    )
    replies = lax.all_to_all(
        result.reshape(expert_total, slots * pieces, block), ("role", "dev"), 0, 0, tiled=True
    )
    mix = gate_values / jnp.sum(gate_values, axis=-1, keepdims=True)
    mix = jnp.broadcast_to(mix[None], (pieces, rows, top)).reshape(pieces * rows, top)
    mixer = jnp.zeros((pieces * rows, places), F32)
    for k in range(top):
        here = jnp.arange(places, dtype=jnp.int32)[None, :] == spot[:, k][:, None]
        mixer = mixer + jnp.where(here, mix[:, k][:, None], 0.0)
    rounded = lax.reduce_precision(mixer, exponent_bits=8, mantissa_bits=7)
    high = rounded.astype(BF16)
    low = (mixer - rounded).astype(BF16)
    both = jnp.dot(
        jnp.concatenate([high, low], axis=0),
        replies.reshape(places, block),
        preferred_element_type=F32,
    )
    mixed = hidden + (both[: pieces * rows] + both[pieces * rows :]).reshape(pieces, rows, block)
    return mixed.astype(BF16).transpose(1, 0, 2).reshape(rows, width)


def solution(mesh):
    both = ("role", "dev")
    return jax.shard_map(
        shards,
        mesh=mesh,
        in_specs=(
            P(both, None),
            P(both, None),
            P(both, None, None, None),
            P(both, None, None, None),
            P(both),
            P("dev", None),
            P(),
            P(both, None),
            P(both, None),
            P(both, None, None),
            P(both, None, None),
            P(both, None, None),
        ),
        out_specs=P(both, None),
        check_vma=False,
    )
```

```python
import functools
import math

import jax
import jax.numpy as jnp
import numpy as np
from jax import lax
from jax.experimental import pallas as pl
from jax.experimental.pallas import tpu as pltpu
from jax.sharding import PartitionSpec as P

BF16 = jnp.bfloat16
F32 = jnp.float32


def sign_table(order):
    signs = np.ones((1, 1), np.float32)
    while signs.shape[0] < order:
        signs = np.block([[signs, signs], [signs, -signs]])
    return signs


def attend_kernel(copies, len_ref, q_ref, k_ref, v_ref, table_ref, out_ref):
    rows, _, cache_len, dim = k_ref.shape
    heads = q_ref.shape[1] // dim
    total = rows * heads
    at = lax.broadcasted_iota(jnp.int32, (total, total), 0)
    to = lax.broadcasted_iota(jnp.int32, (total, total), 1)
    turn_in = (to == (at % heads) * rows + at // heads).astype(F32).astype(BF16)
    turn_out = (to == (at % rows) * heads + at // rows).astype(F32).astype(BF16)
    stacked = jnp.concatenate([q_ref[:, h * dim:(h + 1) * dim] for h in range(heads)], axis=0)
    q = jnp.dot(turn_in, stacked, preferred_element_type=F32).astype(BF16)
    position = lax.broadcasted_iota(jnp.int32, (heads, cache_len), 1)
    scores = []
    for r in range(rows):
        s = lax.dot_general(
            q[r * heads:(r + 1) * heads], k_ref[r, 0], (((1,), (1,)), ((), ())), preferred_element_type=F32
        )
        scores.append(jnp.where(position < len_ref[r], s * (1.0 / math.sqrt(dim)), -1e30))
    scores = jnp.concatenate(scores, axis=0)
    weights = jnp.exp(scores - jnp.max(scores, axis=-1, keepdims=True))
    probs = (weights / jnp.sum(weights, axis=-1, keepdims=True)).astype(BF16)
    rotated = jnp.concatenate(
        [
            jnp.dot(probs[r * heads:(r + 1) * heads], v_ref[r, 0], preferred_element_type=F32).astype(BF16)
            for r in range(rows)
        ],
        axis=0,
    )
    turned = jnp.dot(turn_out, rotated, preferred_element_type=F32).astype(BF16)
    context = jnp.dot(turned, table_ref[...], preferred_element_type=F32) * (1.0 / math.sqrt(dim))
    context = context.astype(BF16)
    each = out_ref.shape[3] // dim
    for h in range(heads):
        piece = context[h * rows:(h + 1) * rows]
        for c in range(copies):
            out_ref[h // each, c, :, (h % each) * dim:(h % each + 1) * dim] = piece


def attend(lengths, queries, key_cache, value_cache, clusters, copies):
    rows, kv_heads, cache_len, dim = key_cache.shape
    share = queries.shape[1] // kv_heads
    columns = queries.shape[1] // clusters
    table = jnp.asarray(sign_table(dim), BF16)
    per = clusters // kv_heads
    return pl.pallas_call(
        functools.partial(attend_kernel, copies),
        grid=(kv_heads,),
        out_shape=jax.ShapeDtypeStruct((clusters, copies, rows, columns), BF16),
        in_specs=[
            pl.BlockSpec(memory_space=pltpu.SMEM),
            pl.BlockSpec((rows, share), lambda i: (0, i)),
            pl.BlockSpec((rows, 1, cache_len, dim), lambda i: (0, i, 0, 0)),
            pl.BlockSpec((rows, 1, cache_len, dim), lambda i: (0, i, 0, 0)),
            pl.BlockSpec((dim, dim), lambda i: (0, 0)),
        ],
        out_specs=pl.BlockSpec((per, copies, rows, columns), lambda i: (i, 0, 0, 0)),
        compiler_params=pltpu.CompilerParams(vmem_limit_bytes=24 * 1024 * 1024),
        cost_estimate=pl.CostEstimate(
            flops=4 * rows * queries.shape[1] * cache_len,
            bytes_accessed=4 * rows * kv_heads * cache_len * dim + 2 * clusters * copies * rows * columns,
            transcendentals=rows * queries.shape[1] // dim * cache_len,
        ),
    )(lengths, queries, key_cache, value_cache, table)


def expert_kernel(pieces, x_ref, gate_ref, up_hbm, down_hbm, out_hbm,
                  up_ref, down_ref, x_s, act_s, res_s, out_s, w_sem, o_sem):
    group, block = x_ref.shape[1:]
    span = group // pieces
    fetch_up = pltpu.make_async_copy(up_hbm, up_ref, w_sem.at[0])
    fetch_down = pltpu.make_async_copy(down_hbm, down_ref, w_sem.at[1])
    fetch_up.start()
    fetch_down.start()
    row = lax.broadcasted_iota(jnp.int32, (group, group), 0)
    col = lax.broadcasted_iota(jnp.int32, (group, group), 1)
    spread = (col == (row % span) * pieces + row // span).astype(F32).astype(BF16)
    gather = (row == (col % span) * pieces + col // span).astype(F32).astype(BF16)
    for g in range(x_ref.shape[0]):
        y = jnp.dot(spread, x_ref[g], preferred_element_type=F32).astype(BF16)
        for j in range(pieces):
            x_s[g * span:(g + 1) * span, j * block:(j + 1) * block] = y[j * span:(j + 1) * span, :]
    gate = jnp.dot(x_s[...], gate_ref[...], preferred_element_type=F32)
    gate = gate / (1.0 + jnp.exp(-gate))
    fetch_up.wait()
    up = jnp.dot(x_s[...], up_ref[...], preferred_element_type=F32)
    act_s[...] = (gate * up).astype(BF16)
    fetch_down.wait()
    tall = 2 * block
    for i in range(down_ref.shape[1] // tall):
        y = jnp.dot(act_s[...], down_ref[:, i * tall:(i + 1) * tall], preferred_element_type=F32).astype(BF16)
        for n in range(2):
            j = i * 2 + n
            for g in range(x_ref.shape[0]):
                res_s[g, j * span:(j + 1) * span, :] = y[g * span:(g + 1) * span, n * block:(n + 1) * block]
    stores = []
    for g in range(x_ref.shape[0]):
        out_s[g] = jnp.dot(gather, res_s[g], preferred_element_type=F32).astype(BF16)
        store = pltpu.make_async_copy(out_s.at[g], out_hbm.at[g], o_sem.at[g])
        store.start()
        stores.append(store)
    for store in stores:
        store.wait()


def experts(x, w_gate, w_up, w_down, pieces):
    rows, block = x.shape
    width, hidden = w_gate.shape
    tokens = rows // pieces
    groups = pieces
    group = rows // groups
    operands = [
        pltpu.with_memory_space_constraint(a, pltpu.VMEM)
        for a in (x.reshape(groups, group, block), w_gate)
    ] + [w_up, w_down]
    result = pl.pallas_call(
        functools.partial(expert_kernel, pieces),
        out_shape=jax.ShapeDtypeStruct((groups, group, block), BF16),
        in_specs=[pl.BlockSpec(memory_space=pltpu.VMEM)] * 2 + [pl.BlockSpec(memory_space=pl.ANY)] * 2,
        out_specs=pl.BlockSpec(memory_space=pl.ANY),
        scratch_shapes=[
            pltpu.VMEM((width, hidden), BF16),
            pltpu.VMEM((hidden, width), BF16),
            pltpu.VMEM((tokens, width), BF16),
            pltpu.VMEM((tokens, hidden), BF16),
            pltpu.VMEM((groups, group, block), BF16),
            pltpu.VMEM((groups, group, block), BF16),
            pltpu.SemaphoreType.DMA((2,)),
            pltpu.SemaphoreType.DMA((groups,)),
        ],
        compiler_params=pltpu.CompilerParams(vmem_limit_bytes=40 * 1024 * 1024),
        cost_estimate=pl.CostEstimate(
            flops=6 * tokens * width * hidden,
            bytes_accessed=4 * width * hidden + 4 * rows * block,
            transcendentals=tokens * hidden,
        ),
    )(*operands)
    return result.reshape(rows, block)


def project_kernel(a_ref, w_ref, out_ref):
    out_ref[...] = jnp.dot(a_ref[...], w_ref[...], preferred_element_type=F32).astype(BF16)


def project(a, w):
    rows, depth = a.shape
    columns = w.shape[1]
    tile = 256
    return pl.pallas_call(
        project_kernel,
        grid=(rows // tile,),
        out_shape=jax.ShapeDtypeStruct((rows, columns), BF16),
        in_specs=[
            pl.BlockSpec((tile, depth), lambda i: (i, 0)),
            pl.BlockSpec((depth, columns), lambda i: (0, 0)),
        ],
        out_specs=pl.BlockSpec((tile, columns), lambda i: (i, 0)),
        compiler_params=pltpu.CompilerParams(vmem_limit_bytes=24 * 1024 * 1024),
        cost_estimate=pl.CostEstimate(
            flops=2 * rows * depth * columns,
            bytes_accessed=2 * (rows * depth + depth * columns + rows * columns),
            transcendentals=0,
        ),
    )(a, w)


def shards(
    residual_in,
    queries,
    key_cache,
    value_cache,
    lengths,
    out_weight,
    norm_gain,
    expert_ids,
    gate_values,
    w_gate,
    w_up,
    w_down,
):
    rows = queries.shape[0]
    head_dim = key_cache.shape[3]
    width = residual_in.shape[1]
    chips = lax.axis_size("dev")
    pieces = 8
    clusters = chips // pieces
    block = width // pieces

    teams = [[c * pieces + i for i in range(pieces)] for c in range(clusters)]
    weight = out_weight.reshape(out_weight.shape[0], pieces, block).transpose(1, 0, 2)
    weight = lax.all_to_all(weight, "dev", 0, 0, tiled=True, axis_index_groups=teams)
    weight = weight.reshape(pieces * out_weight.shape[0], block)

    context = attend(lengths, queries, key_cache, value_cache, clusters, pieces)
    context = context.reshape(chips, rows, pieces * head_dim)
    context = lax.all_to_all(context, "dev", 0, 0, tiled=True)
    part = project(context.reshape(chips * rows, pieces * head_dim), weight)
    part = lax.all_to_all(part.reshape(chips, rows, block), "dev", 0, 0, tiled=True)
    attn = jnp.sum(part.reshape(clusters, pieces, rows, block).astype(F32), axis=0)

    residual = residual_in.reshape(rows, pieces, block).transpose(1, 0, 2)
    hidden = residual.astype(F32) + attn
    scale = lax.rsqrt(jnp.sum(hidden * hidden, axis=(0, 2), keepdims=True) / width + 1e-06)
    normed = (hidden * scale * norm_gain.reshape(pieces, 1, block)).astype(BF16)
    normed = normed.reshape(pieces * rows, block)

    top = expert_ids.shape[1]
    expert_total = chips * lax.axis_size("role")
    slots = 2
    pairs = rows * top
    flat = expert_ids.reshape(pairs)
    same = flat[:, None] == flat[None, :]
    before = jnp.arange(pairs)[:, None] > jnp.arange(pairs)[None, :]
    slot = jnp.sum((same & before).astype(jnp.int32), axis=1)
    target = (flat * slots + slot).reshape(rows, top)
    places = expert_total * slots * pieces
    spot = target[None] * pieces + jnp.arange(pieces, dtype=jnp.int32)[:, None, None]
    spot = spot.reshape(pieces * rows, top)
    chosen = jnp.zeros((places, pieces * rows), jnp.bool_)
    for k in range(top):
        chosen = chosen | (jnp.arange(places, dtype=jnp.int32)[:, None] == spot[:, k][None, :])
    outgoing = jnp.dot(chosen.astype(BF16), normed, preferred_element_type=F32).astype(BF16)
    arrived = lax.all_to_all(
        outgoing.reshape(expert_total, slots * pieces, block), ("role", "dev"), 0, 0, tiled=True
    )
    result = experts(
        arrived.reshape(places, block), w_gate[0], w_up[0], w_down[0], pieces
    )
    replies = lax.all_to_all(
        result.reshape(expert_total, slots * pieces, block), ("role", "dev"), 0, 0, tiled=True
    )
    mix = gate_values / jnp.sum(gate_values, axis=-1, keepdims=True)
    mix = jnp.broadcast_to(mix[None], (pieces, rows, top)).reshape(pieces * rows, top)
    mixer = jnp.zeros((pieces * rows, places), F32)
    for k in range(top):
        here = jnp.arange(places, dtype=jnp.int32)[None, :] == spot[:, k][:, None]
        mixer = mixer + jnp.where(here, mix[:, k][:, None], 0.0)
    rounded = lax.reduce_precision(mixer, exponent_bits=8, mantissa_bits=7)
    high = rounded.astype(BF16)
    low = (mixer - rounded).astype(BF16)
    both = jnp.dot(
        jnp.concatenate([high, low], axis=0),
        replies.reshape(places, block),
        preferred_element_type=F32,
    )
    mixed = hidden + (both[: pieces * rows] + both[pieces * rows :]).reshape(pieces, rows, block)
    return mixed.astype(BF16).transpose(1, 0, 2).reshape(rows, width)


def solution(mesh):
    both = ("role", "dev")
    return jax.shard_map(
        shards,
        mesh=mesh,
        in_specs=(
            P(both, None),
            P(both, None),
            P(both, None, None, None),
            P(both, None, None, None),
            P(both),
            P("dev", None),
            P(),
            P(both, None),
            P(both, None),
            P(both, None, None),
            P(both, None, None),
            P(both, None, None),
        ),
        out_specs=P(both, None),
        check_vma=False,
    )
```

```python
import functools
import math

import jax
import jax.numpy as jnp
import numpy as np
from jax import lax
from jax.experimental import pallas as pl
from jax.experimental.pallas import tpu as pltpu
from jax.sharding import PartitionSpec as P

BF16 = jnp.bfloat16
F32 = jnp.float32


def in_hbm(x):
    return pltpu.with_memory_space_constraint(x, pltpu.HBM)


def sign_table(order):
    signs = np.ones((1, 1), np.float32)
    while signs.shape[0] < order:
        signs = np.block([[signs, signs], [signs, -signs]])
    return signs


def attend_kernel(copies, len_ref, q_ref, k_ref, v_ref, table_ref, out_ref):
    rows, _, cache_len, dim = k_ref.shape
    heads = q_ref.shape[1] // dim
    total = rows * heads
    at = lax.broadcasted_iota(jnp.int32, (total, total), 0)
    to = lax.broadcasted_iota(jnp.int32, (total, total), 1)
    turn_in = (to == (at % heads) * rows + at // heads).astype(F32).astype(BF16)
    turn_out = (to == (at % rows) * heads + at // rows).astype(F32).astype(BF16)
    stacked = jnp.concatenate([q_ref[:, h * dim:(h + 1) * dim] for h in range(heads)], axis=0)
    q = jnp.dot(turn_in, stacked, preferred_element_type=F32).astype(BF16)
    position = lax.broadcasted_iota(jnp.int32, (heads, cache_len), 1)
    scores = []
    for r in range(rows):
        s = lax.dot_general(
            q[r * heads:(r + 1) * heads], k_ref[r, 0], (((1,), (1,)), ((), ())), preferred_element_type=F32
        )
        scores.append(jnp.where(position < len_ref[r], s * (1.0 / math.sqrt(dim)), -1e30))
    scores = jnp.concatenate(scores, axis=0)
    weights = jnp.exp(scores - jnp.max(scores, axis=-1, keepdims=True))
    probs = (weights / jnp.sum(weights, axis=-1, keepdims=True)).astype(BF16)
    rotated = jnp.concatenate(
        [
            jnp.dot(probs[r * heads:(r + 1) * heads], v_ref[r, 0], preferred_element_type=F32).astype(BF16)
            for r in range(rows)
        ],
        axis=0,
    )
    turned = jnp.dot(turn_out, rotated, preferred_element_type=F32).astype(BF16)
    context = jnp.dot(turned, table_ref[...], preferred_element_type=F32) * (1.0 / math.sqrt(dim))
    context = context.astype(BF16)
    each = out_ref.shape[3] // dim
    for h in range(heads):
        piece = context[h * rows:(h + 1) * rows]
        for c in range(copies):
            out_ref[h // each, c, :, (h % each) * dim:(h % each + 1) * dim] = piece


def attend(lengths, queries, key_cache, value_cache, clusters, copies):
    rows, kv_heads, cache_len, dim = key_cache.shape
    share = queries.shape[1] // kv_heads
    columns = queries.shape[1] // clusters
    table = jnp.asarray(sign_table(dim), BF16)
    per = clusters // kv_heads
    return pl.pallas_call(
        functools.partial(attend_kernel, copies),
        grid=(kv_heads,),
        out_shape=pltpu.HBM((clusters, copies, rows, columns), BF16),
        in_specs=[
            pl.BlockSpec(memory_space=pltpu.SMEM),
            pl.BlockSpec((rows, share), lambda i: (0, i)),
            pl.BlockSpec((rows, 1, cache_len, dim), lambda i: (0, i, 0, 0)),
            pl.BlockSpec((rows, 1, cache_len, dim), lambda i: (0, i, 0, 0)),
            pl.BlockSpec((dim, dim), lambda i: (0, 0)),
        ],
        out_specs=pl.BlockSpec((per, copies, rows, columns), lambda i: (i, 0, 0, 0)),
        compiler_params=pltpu.CompilerParams(vmem_limit_bytes=60 * 1024 * 1024),
        cost_estimate=pl.CostEstimate(
            flops=4 * rows * queries.shape[1] * cache_len,
            bytes_accessed=4 * rows * kv_heads * cache_len * dim + 2 * clusters * copies * rows * columns,
            transcendentals=rows * queries.shape[1] // dim * cache_len,
        ),
    )(lengths, queries, in_hbm(key_cache), in_hbm(value_cache), table)


def expert_kernel(pieces, x_ref, gate_ref, up_hbm, down_hbm, out_hbm,
                  up_ref, down_ref, x_s, act_s, res_s, out_s, w_sem, o_sem):
    group, block = x_ref.shape[1:]
    span = group // pieces
    fetch_up = pltpu.make_async_copy(up_hbm, up_ref, w_sem.at[0])
    fetch_down = pltpu.make_async_copy(down_hbm, down_ref, w_sem.at[1])
    fetch_up.start()
    fetch_down.start()
    row = lax.broadcasted_iota(jnp.int32, (group, group), 0)
    col = lax.broadcasted_iota(jnp.int32, (group, group), 1)
    spread = (col == (row % span) * pieces + row // span).astype(F32).astype(BF16)
    gather = (row == (col % span) * pieces + col // span).astype(F32).astype(BF16)
    for g in range(x_ref.shape[0]):
        y = jnp.dot(spread, x_ref[g], preferred_element_type=F32).astype(BF16)
        for j in range(pieces):
            x_s[g * span:(g + 1) * span, j * block:(j + 1) * block] = y[j * span:(j + 1) * span, :]
    gate = jnp.dot(x_s[...], gate_ref[...], preferred_element_type=F32)
    gate = gate / (1.0 + jnp.exp(-gate))
    fetch_up.wait()
    up = jnp.dot(x_s[...], up_ref[...], preferred_element_type=F32)
    act_s[...] = (gate * up).astype(BF16)
    fetch_down.wait()
    tall = 2 * block
    for i in range(down_ref.shape[1] // tall):
        y = jnp.dot(act_s[...], down_ref[:, i * tall:(i + 1) * tall], preferred_element_type=F32).astype(BF16)
        for n in range(2):
            j = i * 2 + n
            for g in range(x_ref.shape[0]):
                res_s[g, j * span:(j + 1) * span, :] = y[g * span:(g + 1) * span, n * block:(n + 1) * block]
    stores = []
    for g in range(x_ref.shape[0]):
        out_s[g] = jnp.dot(gather, res_s[g], preferred_element_type=F32).astype(BF16)
        store = pltpu.make_async_copy(out_s.at[g], out_hbm.at[g], o_sem.at[g])
        store.start()
        stores.append(store)
    for store in stores:
        store.wait()


def experts(x, w_gate, w_up, w_down, pieces):
    rows, block = x.shape
    width, hidden = w_gate.shape
    tokens = rows // pieces
    groups = pieces
    group = rows // groups
    operands = [
        pltpu.with_memory_space_constraint(a, pltpu.VMEM)
        for a in (x.reshape(groups, group, block), w_gate)
    ] + [in_hbm(w_up), in_hbm(w_down)]
    result = pl.pallas_call(
        functools.partial(expert_kernel, pieces),
        out_shape=pltpu.HBM((groups, group, block), BF16),
        in_specs=[pl.BlockSpec(memory_space=pltpu.VMEM)] * 2 + [pl.BlockSpec(memory_space=pltpu.HBM)] * 2,
        out_specs=pl.BlockSpec(memory_space=pltpu.HBM),
        scratch_shapes=[
            pltpu.VMEM((width, hidden), BF16),
            pltpu.VMEM((hidden, width), BF16),
            pltpu.VMEM((tokens, width), BF16),
            pltpu.VMEM((tokens, hidden), BF16),
            pltpu.VMEM((groups, group, block), BF16),
            pltpu.VMEM((groups, group, block), BF16),
            pltpu.SemaphoreType.DMA((2,)),
            pltpu.SemaphoreType.DMA((groups,)),
        ],
        compiler_params=pltpu.CompilerParams(vmem_limit_bytes=40 * 1024 * 1024),
        cost_estimate=pl.CostEstimate(
            flops=6 * tokens * width * hidden,
            bytes_accessed=4 * width * hidden + 4 * rows * block,
            transcendentals=tokens * hidden,
        ),
    )(*operands)
    return result.reshape(rows, block)


def project_kernel(me_ref, a_ref, mine_hbm, other_hbm, out_hbm, w_s, out_s, w_sem, o_sem):
    members, half, _ = mine_hbm.shape
    tiles, tile, _ = out_s.shape
    moves = []
    for n, source in enumerate((mine_hbm, other_hbm)):
        first = me_ref[0] if n == 0 else 1 - me_ref[0]
        for m in range(members):
            at = pl.multiple_of((2 * m + first) * half, half)
            moves.append(pltpu.make_async_copy(source.at[m], w_s.at[pl.ds(at, half)], w_sem.at[n, m]))
    for move in moves:
        move.start()
    for move in moves:
        move.wait()
    stores = []
    for t in range(tiles):
        out_s[t] = jnp.dot(
            a_ref[t * tile:(t + 1) * tile, :], w_s[...], preferred_element_type=F32
        ).astype(BF16)
        stores.append(pltpu.make_async_copy(out_s.at[t], out_hbm.at[t], o_sem.at[t]))
        stores[-1].start()
    for store in stores:
        store.wait()


def project(me, a, mine, other):
    rows, depth = a.shape
    members, half, columns = mine.shape
    tiles = 4
    result = pl.pallas_call(
        project_kernel,
        out_shape=pltpu.HBM((tiles, rows // tiles, columns), BF16),
        in_specs=[
            pl.BlockSpec(memory_space=pltpu.SMEM),
            pl.BlockSpec(memory_space=pltpu.VMEM),
            pl.BlockSpec(memory_space=pltpu.HBM),
            pl.BlockSpec(memory_space=pltpu.HBM),
        ],
        out_specs=pl.BlockSpec(memory_space=pltpu.HBM),
        scratch_shapes=[
            pltpu.VMEM((depth, columns), BF16),
            pltpu.VMEM((tiles, rows // tiles, columns), BF16),
            pltpu.SemaphoreType.DMA((2, members)),
            pltpu.SemaphoreType.DMA((tiles,)),
        ],
        compiler_params=pltpu.CompilerParams(vmem_limit_bytes=12 * 1024 * 1024),
        cost_estimate=pl.CostEstimate(
            flops=2 * rows * depth * columns,
            bytes_accessed=2 * (rows * depth + depth * columns + rows * columns),
            transcendentals=0,
        ),
    )(me, pltpu.with_memory_space_constraint(a, pltpu.VMEM), in_hbm(mine), in_hbm(other))
    return result.reshape(rows, columns)


def shards(
    residual_in,
    queries,
    key_cache,
    value_cache,
    lengths,
    out_weight,
    norm_gain,
    expert_ids,
    gate_values,
    w_gate,
    w_up,
    w_down,
):
    rows = queries.shape[0]
    head_dim = key_cache.shape[3]
    width = residual_in.shape[1]
    chips = lax.axis_size("dev")
    pieces = 8
    clusters = chips // pieces
    block = width // pieces

    teams = [[c * pieces + i for i in range(pieces)] for c in range(clusters)]
    core = lax.axis_index("role").astype(jnp.int32)
    half = out_weight.shape[0] // 2
    mine = lax.dynamic_slice_in_dim(out_weight, core * half, half, 0)
    mine = mine.reshape(half, pieces, block).transpose(1, 0, 2)
    mine = lax.all_to_all(mine, "dev", 0, 0, tiled=True, axis_index_groups=teams)
    other = lax.ppermute(mine, "role", [(0, 1), (1, 0)])

    context = attend(lengths, queries, key_cache, value_cache, clusters, pieces)
    context = context.reshape(chips, rows, pieces * head_dim)
    context = lax.all_to_all(context, "dev", 0, 0, tiled=True)
    part = project(core.reshape(1), context.reshape(chips * rows, pieces * head_dim), mine, other)
    part = lax.all_to_all(part.reshape(chips, rows, block), "dev", 0, 0, tiled=True)
    attn = jnp.sum(part.reshape(clusters, pieces, rows, block).astype(F32), axis=0)

    residual = residual_in.reshape(rows, pieces, block).transpose(1, 0, 2)
    hidden = residual.astype(F32) + attn
    scale = lax.rsqrt(jnp.sum(hidden * hidden, axis=(0, 2), keepdims=True) / width + 1e-06)
    normed = (hidden * scale * norm_gain.reshape(pieces, 1, block)).astype(BF16)
    normed = normed.reshape(pieces * rows, block)

    top = expert_ids.shape[1]
    expert_total = chips * lax.axis_size("role")
    slots = 2
    pairs = rows * top
    flat = expert_ids.reshape(pairs)
    same = flat[:, None] == flat[None, :]
    before = jnp.arange(pairs)[:, None] > jnp.arange(pairs)[None, :]
    slot = jnp.sum((same & before).astype(jnp.int32), axis=1)
    target = (flat * slots + slot).reshape(rows, top)
    places = expert_total * slots * pieces
    spot = target[None] * pieces + jnp.arange(pieces, dtype=jnp.int32)[:, None, None]
    spot = spot.reshape(pieces * rows, top)
    chosen = jnp.zeros((places, pieces * rows), jnp.bool_)
    for k in range(top):
        chosen = chosen | (jnp.arange(places, dtype=jnp.int32)[:, None] == spot[:, k][None, :])
    outgoing = jnp.dot(chosen.astype(BF16), normed, preferred_element_type=F32).astype(BF16)
    arrived = lax.all_to_all(
        outgoing.reshape(expert_total, slots * pieces, block), ("role", "dev"), 0, 0, tiled=True
    )
    result = experts(
        arrived.reshape(places, block), w_gate[0], w_up[0], w_down[0], pieces
    )
    replies = lax.all_to_all(
        result.reshape(expert_total, slots * pieces, block), ("role", "dev"), 0, 0, tiled=True
    )
    mix = gate_values / jnp.sum(gate_values, axis=-1, keepdims=True)
    mix = jnp.broadcast_to(mix[None], (pieces, rows, top)).reshape(pieces * rows, top)
    mixer = jnp.zeros((pieces * rows, places), F32)
    for k in range(top):
        here = jnp.arange(places, dtype=jnp.int32)[None, :] == spot[:, k][:, None]
        mixer = mixer + jnp.where(here, mix[:, k][:, None], 0.0)
    rounded = lax.reduce_precision(mixer, exponent_bits=8, mantissa_bits=7)
    high = rounded.astype(BF16)
    low = (mixer - rounded).astype(BF16)
    both = jnp.dot(
        jnp.concatenate([high, low], axis=0),
        replies.reshape(places, block),
        preferred_element_type=F32,
    )
    mixed = hidden + (both[: pieces * rows] + both[pieces * rows :]).reshape(pieces, rows, block)
    return mixed.astype(BF16).transpose(1, 0, 2).reshape(rows, width)


def solution(mesh):
    both = ("role", "dev")
    return jax.shard_map(
        shards,
        mesh=mesh,
        in_specs=(
            P(both, None),
            P(both, None),
            P(both, None, None, None),
            P(both, None, None, None),
            P(both),
            P("dev", None),
            P(),
            P(both, None),
            P(both, None),
            P(both, None, None),
            P(both, None, None),
            P(both, None, None),
        ),
        out_specs=P(both, None),
        check_vma=False,
    )
```

```python
import functools
import math

import jax
import jax.numpy as jnp
import numpy as np
from jax import lax
from jax.experimental import pallas as pl
from jax.experimental.pallas import tpu as pltpu
from jax.sharding import PartitionSpec as P

BF16 = jnp.bfloat16
F32 = jnp.float32


def in_hbm(x):
    return pltpu.with_memory_space_constraint(x, pltpu.HBM)


def sign_table(order):
    signs = np.ones((1, 1), np.float32)
    while signs.shape[0] < order:
        signs = np.block([[signs, signs], [signs, -signs]])
    return signs


def attend_kernel(copies, len_ref, q_ref, k_ref, v_ref, table_ref, out_ref):
    rows, _, cache_len, dim = k_ref.shape
    heads = q_ref.shape[1] // dim
    total = rows * heads
    at = lax.broadcasted_iota(jnp.int32, (total, total), 0)
    to = lax.broadcasted_iota(jnp.int32, (total, total), 1)
    turn_in = (to == (at % heads) * rows + at // heads).astype(F32).astype(BF16)
    turn_out = (to == (at % rows) * heads + at // rows).astype(F32).astype(BF16)
    stacked = jnp.concatenate([q_ref[:, h * dim:(h + 1) * dim] for h in range(heads)], axis=0)
    q = jnp.dot(turn_in, stacked, preferred_element_type=F32).astype(BF16)
    position = lax.broadcasted_iota(jnp.int32, (heads, cache_len), 1)
    scores = []
    for r in range(rows):
        s = lax.dot_general(
            q[r * heads:(r + 1) * heads], k_ref[r, 0], (((1,), (1,)), ((), ())), preferred_element_type=F32
        )
        scores.append(jnp.where(position < len_ref[r], s * (1.0 / math.sqrt(dim)), -1e30))
    scores = jnp.concatenate(scores, axis=0)
    weights = jnp.exp(scores - jnp.max(scores, axis=-1, keepdims=True))
    probs = (weights / jnp.sum(weights, axis=-1, keepdims=True)).astype(BF16)
    rotated = jnp.concatenate(
        [
            jnp.dot(probs[r * heads:(r + 1) * heads], v_ref[r, 0], preferred_element_type=F32).astype(BF16)
            for r in range(rows)
        ],
        axis=0,
    )
    turned = jnp.dot(turn_out, rotated, preferred_element_type=F32).astype(BF16)
    context = jnp.dot(turned, table_ref[...], preferred_element_type=F32) * (1.0 / math.sqrt(dim))
    context = context.astype(BF16)
    each = out_ref.shape[3] // dim
    for h in range(heads):
        piece = context[h * rows:(h + 1) * rows]
        for c in range(copies):
            out_ref[h // each, c, :, (h % each) * dim:(h % each + 1) * dim] = piece


def attend(lengths, queries, key_cache, value_cache, clusters, copies):
    rows, kv_heads, cache_len, dim = key_cache.shape
    share = queries.shape[1] // kv_heads
    columns = queries.shape[1] // clusters
    table = jnp.asarray(sign_table(dim), BF16)
    per = clusters // kv_heads
    return pl.pallas_call(
        functools.partial(attend_kernel, copies),
        grid=(kv_heads,),
        out_shape=pltpu.HBM((clusters, copies, rows, columns), BF16),
        in_specs=[
            pl.BlockSpec(memory_space=pltpu.SMEM),
            pl.BlockSpec((rows, share), lambda i: (0, i)),
            pl.BlockSpec((rows, 1, cache_len, dim), lambda i: (0, i, 0, 0)),
            pl.BlockSpec((rows, 1, cache_len, dim), lambda i: (0, i, 0, 0)),
            pl.BlockSpec((dim, dim), lambda i: (0, 0)),
        ],
        out_specs=pl.BlockSpec((per, copies, rows, columns), lambda i: (i, 0, 0, 0)),
        compiler_params=pltpu.CompilerParams(vmem_limit_bytes=60 * 1024 * 1024),
        cost_estimate=pl.CostEstimate(
            flops=4 * rows * queries.shape[1] * cache_len,
            bytes_accessed=4 * rows * kv_heads * cache_len * dim + 2 * clusters * copies * rows * columns,
            transcendentals=rows * queries.shape[1] // dim * cache_len,
        ),
    )(lengths, queries, in_hbm(key_cache), in_hbm(value_cache), table)


WIDE, TALL, AHEAD = 384, 2048, 2


def expert_kernel(pieces, x_ref, gate_hbm, up_hbm, down_hbm, out_hbm,
                  gate_s, up_s, down_s, x_s, act_s, res_s, out_s, w_sem, d_sem, o_sem):
    group, block = x_ref.shape[1:]
    span = group // pieces
    parts, _, wide = gate_s.shape
    outs, _, tall = down_s.shape
    loads = []
    for i in range(parts):
        cut = pl.ds(i * wide, wide)
        loads.append(pltpu.make_async_copy(gate_hbm.at[:, cut], gate_s.at[i], w_sem.at[i, 0]))
        loads.append(pltpu.make_async_copy(up_hbm.at[:, cut], up_s.at[i], w_sem.at[i, 1]))
    for i in range(outs):
        loads.append(pltpu.make_async_copy(down_hbm.at[:, pl.ds(i * tall, tall)], down_s.at[i], d_sem.at[i]))

    def arrive(n):
        loads[n].wait()
        if n + AHEAD < len(loads):
            loads[n + AHEAD].start()

    for first in loads[:AHEAD]:
        first.start()
    row = lax.broadcasted_iota(jnp.int32, (group, group), 0)
    col = lax.broadcasted_iota(jnp.int32, (group, group), 1)
    spread = (col == (row % span) * pieces + row // span).astype(F32).astype(BF16)
    gather = (row == (col % span) * pieces + col // span).astype(F32).astype(BF16)
    for g in range(x_ref.shape[0]):
        y = jnp.dot(spread, x_ref[g], preferred_element_type=F32).astype(BF16)
        for j in range(pieces):
            x_s[g * span:(g + 1) * span, j * block:(j + 1) * block] = y[j * span:(j + 1) * span, :]
    for i in range(parts):
        arrive(2 * i)
        gate = jnp.dot(x_s[...], gate_s[i], preferred_element_type=F32)
        arrive(2 * i + 1)
        up = jnp.dot(x_s[...], up_s[i], preferred_element_type=F32)
        act_s[:, i * wide:(i + 1) * wide] = (gate / (1.0 + jnp.exp(-gate)) * up).astype(BF16)
    for i in range(outs):
        arrive(2 * parts + i)
        y = jnp.dot(act_s[...], down_s[i], preferred_element_type=F32).astype(BF16)
        for n in range(tall // block):
            j = i * (tall // block) + n
            for g in range(x_ref.shape[0]):
                res_s[g, j * span:(j + 1) * span, :] = y[g * span:(g + 1) * span, n * block:(n + 1) * block]
    stores = []
    for g in range(x_ref.shape[0]):
        out_s[g] = jnp.dot(gather, res_s[g], preferred_element_type=F32).astype(BF16)
        store = pltpu.make_async_copy(out_s.at[g], out_hbm.at[g], o_sem.at[g])
        store.start()
        stores.append(store)
    for store in stores:
        store.wait()


def experts(x, w_gate, w_up, w_down, pieces):
    rows, block = x.shape
    width, hidden = w_gate.shape
    tokens = rows // pieces
    groups = pieces
    group = rows // groups
    wide, tall = min(WIDE, hidden), min(TALL, width)
    operands = [pltpu.with_memory_space_constraint(x.reshape(groups, group, block), pltpu.VMEM)]
    operands += [in_hbm(w_gate), in_hbm(w_up), in_hbm(w_down)]
    result = pl.pallas_call(
        functools.partial(expert_kernel, pieces),
        out_shape=pltpu.HBM((groups, group, block), BF16),
        in_specs=[pl.BlockSpec(memory_space=pltpu.VMEM)] + [pl.BlockSpec(memory_space=pltpu.HBM)] * 3,
        out_specs=pl.BlockSpec(memory_space=pltpu.HBM),
        scratch_shapes=[
            pltpu.VMEM((hidden // wide, width, wide), BF16),
            pltpu.VMEM((hidden // wide, width, wide), BF16),
            pltpu.VMEM((width // tall, hidden, tall), BF16),
            pltpu.VMEM((tokens, width), BF16),
            pltpu.VMEM((tokens, hidden), BF16),
            pltpu.VMEM((groups, group, block), BF16),
            pltpu.VMEM((groups, group, block), BF16),
            pltpu.SemaphoreType.DMA((hidden // wide, 2)),
            pltpu.SemaphoreType.DMA((width // tall,)),
            pltpu.SemaphoreType.DMA((groups,)),
        ],
        compiler_params=pltpu.CompilerParams(vmem_limit_bytes=48 * 1024 * 1024),
        cost_estimate=pl.CostEstimate(
            flops=6 * tokens * width * hidden,
            bytes_accessed=6 * width * hidden + 4 * rows * block,
            transcendentals=tokens * hidden,
        ),
    )(*operands)
    return result.reshape(rows, block)


def project_kernel(me_ref, a_ref, mine_hbm, other_hbm, out_hbm, w_s, out_s, w_sem, o_sem):
    members, half, _ = mine_hbm.shape
    tiles, tile, _ = out_s.shape
    moves = []
    for n, source in enumerate((mine_hbm, other_hbm)):
        first = me_ref[0] if n == 0 else 1 - me_ref[0]
        for m in range(members):
            at = pl.multiple_of((2 * m + first) * half, half)
            moves.append(pltpu.make_async_copy(source.at[m], w_s.at[pl.ds(at, half)], w_sem.at[n, m]))
    for move in moves:
        move.start()
    for move in moves:
        move.wait()
    stores = []
    for t in range(tiles):
        out_s[t] = jnp.dot(
            a_ref[t * tile:(t + 1) * tile, :], w_s[...], preferred_element_type=F32
        ).astype(BF16)
        stores.append(pltpu.make_async_copy(out_s.at[t], out_hbm.at[t], o_sem.at[t]))
        stores[-1].start()
    for store in stores:
        store.wait()


def project(me, a, mine, other):
    rows, depth = a.shape
    members, half, columns = mine.shape
    tiles = 4
    result = pl.pallas_call(
        project_kernel,
        out_shape=pltpu.HBM((tiles, rows // tiles, columns), BF16),
        in_specs=[
            pl.BlockSpec(memory_space=pltpu.SMEM),
            pl.BlockSpec(memory_space=pltpu.VMEM),
            pl.BlockSpec(memory_space=pltpu.HBM),
            pl.BlockSpec(memory_space=pltpu.HBM),
        ],
        out_specs=pl.BlockSpec(memory_space=pltpu.HBM),
        scratch_shapes=[
            pltpu.VMEM((depth, columns), BF16),
            pltpu.VMEM((tiles, rows // tiles, columns), BF16),
            pltpu.SemaphoreType.DMA((2, members)),
            pltpu.SemaphoreType.DMA((tiles,)),
        ],
        compiler_params=pltpu.CompilerParams(vmem_limit_bytes=12 * 1024 * 1024),
        cost_estimate=pl.CostEstimate(
            flops=2 * rows * depth * columns,
            bytes_accessed=2 * (rows * depth + depth * columns + rows * columns),
            transcendentals=0,
        ),
    )(me, pltpu.with_memory_space_constraint(a, pltpu.VMEM), in_hbm(mine), in_hbm(other))
    return result.reshape(rows, columns)


def shards(
    residual_in,
    queries,
    key_cache,
    value_cache,
    lengths,
    out_weight,
    norm_gain,
    expert_ids,
    gate_values,
    w_gate,
    w_up,
    w_down,
):
    rows = queries.shape[0]
    head_dim = key_cache.shape[3]
    width = residual_in.shape[1]
    chips = lax.axis_size("dev")
    pieces = 8
    clusters = chips // pieces
    block = width // pieces

    teams = [[c * pieces + i for i in range(pieces)] for c in range(clusters)]
    core = lax.axis_index("role").astype(jnp.int32)
    half = out_weight.shape[0] // 2
    mine = lax.dynamic_slice_in_dim(out_weight, core * half, half, 0)
    mine = mine.reshape(half, pieces, block).transpose(1, 0, 2)
    mine = lax.all_to_all(mine, "dev", 0, 0, tiled=True, axis_index_groups=teams)
    other = lax.ppermute(mine, "role", [(0, 1), (1, 0)])

    context = attend(lengths, queries, key_cache, value_cache, clusters, pieces)
    context = context.reshape(chips, rows, pieces * head_dim)
    context = lax.all_to_all(context, "dev", 0, 0, tiled=True)
    part = project(core.reshape(1), context.reshape(chips * rows, pieces * head_dim), mine, other)
    part = lax.all_to_all(part.reshape(chips, rows, block), "dev", 0, 0, tiled=True)
    attn = jnp.sum(part.reshape(clusters, pieces, rows, block).astype(F32), axis=0)

    residual = residual_in.reshape(rows, pieces, block).transpose(1, 0, 2)
    hidden = residual.astype(F32) + attn
    scale = lax.rsqrt(jnp.sum(hidden * hidden, axis=(0, 2), keepdims=True) / width + 1e-06)
    normed = (hidden * scale * norm_gain.reshape(pieces, 1, block)).astype(BF16)
    normed = normed.reshape(pieces * rows, block)

    top = expert_ids.shape[1]
    expert_total = chips * lax.axis_size("role")
    slots = 2
    pairs = rows * top
    flat = expert_ids.reshape(pairs)
    same = flat[:, None] == flat[None, :]
    before = jnp.arange(pairs)[:, None] > jnp.arange(pairs)[None, :]
    slot = jnp.sum((same & before).astype(jnp.int32), axis=1)
    target = (flat * slots + slot).reshape(rows, top)
    places = expert_total * slots * pieces
    spot = target[None] * pieces + jnp.arange(pieces, dtype=jnp.int32)[:, None, None]
    spot = spot.reshape(pieces * rows, top)
    chosen = jnp.zeros((places, pieces * rows), jnp.bool_)
    for k in range(top):
        chosen = chosen | (jnp.arange(places, dtype=jnp.int32)[:, None] == spot[:, k][None, :])
    outgoing = jnp.dot(chosen.astype(BF16), normed, preferred_element_type=F32).astype(BF16)
    arrived = lax.all_to_all(
        outgoing.reshape(expert_total, slots * pieces, block), ("role", "dev"), 0, 0, tiled=True
    )
    result = experts(
        arrived.reshape(places, block), w_gate[0], w_up[0], w_down[0], pieces
    )
    replies = lax.all_to_all(
        result.reshape(expert_total, slots * pieces, block), ("role", "dev"), 0, 0, tiled=True
    )
    mix = gate_values / jnp.sum(gate_values, axis=-1, keepdims=True)
    mix = jnp.broadcast_to(mix[None], (pieces, rows, top)).reshape(pieces * rows, top)
    mixer = jnp.zeros((pieces * rows, places), F32)
    for k in range(top):
        here = jnp.arange(places, dtype=jnp.int32)[None, :] == spot[:, k][:, None]
        mixer = mixer + jnp.where(here, mix[:, k][:, None], 0.0)
    rounded = lax.reduce_precision(mixer, exponent_bits=8, mantissa_bits=7)
    high = rounded.astype(BF16)
    low = (mixer - rounded).astype(BF16)
    both = jnp.dot(
        jnp.concatenate([high, low], axis=0),
        replies.reshape(places, block),
        preferred_element_type=F32,
    )
    mixed = hidden + (both[: pieces * rows] + both[pieces * rows :]).reshape(pieces, rows, block)
    return mixed.astype(BF16).transpose(1, 0, 2).reshape(rows, width)


def solution(mesh):
    both = ("role", "dev")
    return jax.shard_map(
        shards,
        mesh=mesh,
        in_specs=(
            P(both, None),
            P(both, None),
            P(both, None, None, None),
            P(both, None, None, None),
            P(both),
            P("dev", None),
            P(),
            P(both, None),
            P(both, None),
            P(both, None, None),
            P(both, None, None),
            P(both, None, None),
        ),
        out_specs=P(both, None),
        check_vma=False,
    )
```

```python
import functools
import math

import jax
import jax.numpy as jnp
import numpy as np
from jax import lax
from jax.experimental import pallas as pl
from jax.experimental.pallas import tpu as pltpu
from jax.sharding import PartitionSpec as P

BF16 = jnp.bfloat16
F32 = jnp.float32


def in_hbm(x):
    return pltpu.with_memory_space_constraint(x, pltpu.HBM)


def sign_table(order):
    signs = np.ones((1, 1), np.float32)
    while signs.shape[0] < order:
        signs = np.block([[signs, signs], [signs, -signs]])
    return signs


def attend_kernel(copies, len_ref, q_ref, k_ref, v_ref, table_ref, out_ref):
    rows, _, cache_len, dim = k_ref.shape
    heads = q_ref.shape[1] // dim
    total = rows * heads
    at = lax.broadcasted_iota(jnp.int32, (total, total), 0)
    to = lax.broadcasted_iota(jnp.int32, (total, total), 1)
    turn_in = (to == (at % heads) * rows + at // heads).astype(F32).astype(BF16)
    turn_out = (to == (at % rows) * heads + at // rows).astype(F32).astype(BF16)
    stacked = jnp.concatenate([q_ref[:, h * dim:(h + 1) * dim] for h in range(heads)], axis=0)
    q = jnp.dot(turn_in, stacked, preferred_element_type=F32).astype(BF16)
    position = lax.broadcasted_iota(jnp.int32, (heads, cache_len), 1)
    scores = []
    for r in range(rows):
        s = lax.dot_general(
            q[r * heads:(r + 1) * heads], k_ref[r, 0], (((1,), (1,)), ((), ())), preferred_element_type=F32
        )
        scores.append(jnp.where(position < len_ref[r], s * (1.0 / math.sqrt(dim)), -1e30))
    scores = jnp.concatenate(scores, axis=0)
    weights = jnp.exp(scores - jnp.max(scores, axis=-1, keepdims=True))
    probs = (weights / jnp.sum(weights, axis=-1, keepdims=True)).astype(BF16)
    rotated = jnp.concatenate(
        [
            jnp.dot(probs[r * heads:(r + 1) * heads], v_ref[r, 0], preferred_element_type=F32).astype(BF16)
            for r in range(rows)
        ],
        axis=0,
    )
    turned = jnp.dot(turn_out, rotated, preferred_element_type=F32).astype(BF16)
    context = jnp.dot(turned, table_ref[...], preferred_element_type=F32) * (1.0 / math.sqrt(dim))
    context = context.astype(BF16)
    each = out_ref.shape[3] // dim
    for h in range(heads):
        piece = context[h * rows:(h + 1) * rows]
        for c in range(copies):
            out_ref[h // each, c, :, (h % each) * dim:(h % each + 1) * dim] = piece


def attend(lengths, queries, key_cache, value_cache, clusters, copies):
    rows, kv_heads, cache_len, dim = key_cache.shape
    share = queries.shape[1] // kv_heads
    columns = queries.shape[1] // clusters
    table = jnp.asarray(sign_table(dim), BF16)
    per = clusters // kv_heads
    return pl.pallas_call(
        functools.partial(attend_kernel, copies),
        grid=(kv_heads,),
        out_shape=pltpu.HBM((clusters, copies, rows, columns), BF16),
        in_specs=[
            pl.BlockSpec(memory_space=pltpu.SMEM),
            pl.BlockSpec((rows, share), lambda i: (0, i)),
            pl.BlockSpec((rows, 1, cache_len, dim), lambda i: (0, i, 0, 0)),
            pl.BlockSpec((rows, 1, cache_len, dim), lambda i: (0, i, 0, 0)),
            pl.BlockSpec((dim, dim), lambda i: (0, 0)),
        ],
        out_specs=pl.BlockSpec((per, copies, rows, columns), lambda i: (i, 0, 0, 0)),
        compiler_params=pltpu.CompilerParams(vmem_limit_bytes=60 * 1024 * 1024),
        cost_estimate=pl.CostEstimate(
            flops=4 * rows * queries.shape[1] * cache_len,
            bytes_accessed=4 * rows * kv_heads * cache_len * dim + 2 * clusters * copies * rows * columns,
            transcendentals=rows * queries.shape[1] // dim * cache_len,
        ),
    )(lengths, queries, in_hbm(key_cache), in_hbm(value_cache), table)


WIDE, TALL, AHEAD = 384, 2048, 2


def expert_kernel(pieces, x_ref, gate_hbm, up_hbm, down_hbm, out_hbm,
                  gate_s, up_s, down_s, x_s, act_s, res_s, out_s, w_sem, d_sem, o_sem):
    group, block = x_ref.shape[1:]
    span = group // pieces
    parts, _, wide = gate_s.shape
    outs, _, tall = down_s.shape
    loads = []
    for i in range(parts):
        cut = pl.ds(i * wide, wide)
        loads.append(pltpu.make_async_copy(gate_hbm.at[:, cut], gate_s.at[i], w_sem.at[i, 0]))
        loads.append(pltpu.make_async_copy(up_hbm.at[:, cut], up_s.at[i], w_sem.at[i, 1]))
    for i in range(outs):
        loads.append(pltpu.make_async_copy(down_hbm.at[:, pl.ds(i * tall, tall)], down_s.at[i], d_sem.at[i]))

    def arrive(n):
        loads[n].wait()
        if n + AHEAD < len(loads):
            loads[n + AHEAD].start()

    for first in loads[:AHEAD]:
        first.start()
    row = lax.broadcasted_iota(jnp.int32, (group, group), 0)
    col = lax.broadcasted_iota(jnp.int32, (group, group), 1)
    spread = (col == (row % span) * pieces + row // span).astype(F32).astype(BF16)
    gather = (row == (col % span) * pieces + col // span).astype(F32).astype(BF16)
    for g in range(x_ref.shape[0]):
        y = jnp.dot(spread, x_ref[g], preferred_element_type=F32).astype(BF16)
        for j in range(pieces):
            x_s[g * span:(g + 1) * span, j * block:(j + 1) * block] = y[j * span:(j + 1) * span, :]
    for i in range(parts):
        arrive(2 * i)
        gate = jnp.dot(x_s[...], gate_s[i], preferred_element_type=F32)
        arrive(2 * i + 1)
        up = jnp.dot(x_s[...], up_s[i], preferred_element_type=F32)
        act_s[:, i * wide:(i + 1) * wide] = (gate / (1.0 + jnp.exp(-gate)) * up).astype(BF16)
    for i in range(outs):
        arrive(2 * parts + i)
        y = jnp.dot(act_s[...], down_s[i], preferred_element_type=F32).astype(BF16)
        for n in range(tall // block):
            j = i * (tall // block) + n
            for g in range(x_ref.shape[0]):
                res_s[g, j * span:(j + 1) * span, :] = y[g * span:(g + 1) * span, n * block:(n + 1) * block]
    stores = []
    for g in range(x_ref.shape[0]):
        out_s[g] = jnp.dot(gather, res_s[g], preferred_element_type=F32).astype(BF16)
        store = pltpu.make_async_copy(out_s.at[g], out_hbm.at[g], o_sem.at[g])
        store.start()
        stores.append(store)
    for store in stores:
        store.wait()


def experts(x, w_gate, w_up, w_down, pieces):
    rows, block = x.shape
    width, hidden = w_gate.shape
    tokens = rows // pieces
    groups = pieces
    group = rows // groups
    wide, tall = min(WIDE, hidden), min(TALL, width)
    operands = [pltpu.with_memory_space_constraint(x.reshape(groups, group, block), pltpu.VMEM)]
    operands += [in_hbm(w_gate), in_hbm(w_up), in_hbm(w_down)]
    result = pl.pallas_call(
        functools.partial(expert_kernel, pieces),
        out_shape=pltpu.HBM((groups, group, block), BF16),
        in_specs=[pl.BlockSpec(memory_space=pltpu.VMEM)] + [pl.BlockSpec(memory_space=pltpu.HBM)] * 3,
        out_specs=pl.BlockSpec(memory_space=pltpu.HBM),
        scratch_shapes=[
            pltpu.VMEM((hidden // wide, width, wide), BF16),
            pltpu.VMEM((hidden // wide, width, wide), BF16),
            pltpu.VMEM((width // tall, hidden, tall), BF16),
            pltpu.VMEM((tokens, width), BF16),
            pltpu.VMEM((tokens, hidden), BF16),
            pltpu.VMEM((groups, group, block), BF16),
            pltpu.VMEM((groups, group, block), BF16),
            pltpu.SemaphoreType.DMA((hidden // wide, 2)),
            pltpu.SemaphoreType.DMA((width // tall,)),
            pltpu.SemaphoreType.DMA((groups,)),
        ],
        compiler_params=pltpu.CompilerParams(vmem_limit_bytes=48 * 1024 * 1024),
        cost_estimate=pl.CostEstimate(
            flops=6 * tokens * width * hidden,
            bytes_accessed=6 * width * hidden + 4 * rows * block,
            transcendentals=tokens * hidden,
        ),
    )(*operands)
    return result.reshape(rows, block)


def project_kernel(me_ref, a_ref, mine_hbm, other_hbm, out_hbm, w_s, out_s, w_sem, o_sem):
    members, half, _ = mine_hbm.shape
    tiles, tile, _ = out_s.shape
    moves = []
    for n, source in enumerate((mine_hbm, other_hbm)):
        first = me_ref[0] if n == 0 else 1 - me_ref[0]
        for m in range(members):
            at = pl.multiple_of((2 * m + first) * half, half)
            moves.append(pltpu.make_async_copy(source.at[m], w_s.at[pl.ds(at, half)], w_sem.at[n, m]))
    for move in moves:
        move.start()
    for move in moves:
        move.wait()
    stores = []
    for t in range(tiles):
        out_s[t] = jnp.dot(
            a_ref[t * tile:(t + 1) * tile, :], w_s[...], preferred_element_type=F32
        ).astype(BF16)
        stores.append(pltpu.make_async_copy(out_s.at[t], out_hbm.at[t], o_sem.at[t]))
        stores[-1].start()
    for store in stores:
        store.wait()


def project(me, a, mine, other):
    rows, depth = a.shape
    members, half, columns = mine.shape
    tiles = 4
    result = pl.pallas_call(
        project_kernel,
        out_shape=pltpu.HBM((tiles, rows // tiles, columns), BF16),
        in_specs=[
            pl.BlockSpec(memory_space=pltpu.SMEM),
            pl.BlockSpec(memory_space=pltpu.VMEM),
            pl.BlockSpec(memory_space=pltpu.HBM),
            pl.BlockSpec(memory_space=pltpu.HBM),
        ],
        out_specs=pl.BlockSpec(memory_space=pltpu.HBM),
        scratch_shapes=[
            pltpu.VMEM((depth, columns), BF16),
            pltpu.VMEM((tiles, rows // tiles, columns), BF16),
            pltpu.SemaphoreType.DMA((2, members)),
            pltpu.SemaphoreType.DMA((tiles,)),
        ],
        compiler_params=pltpu.CompilerParams(vmem_limit_bytes=12 * 1024 * 1024),
        cost_estimate=pl.CostEstimate(
            flops=2 * rows * depth * columns,
            bytes_accessed=2 * (rows * depth + depth * columns + rows * columns),
            transcendentals=0,
        ),
    )(me, pltpu.with_memory_space_constraint(a, pltpu.VMEM), in_hbm(mine), in_hbm(other))
    return result.reshape(rows, columns)


def shards(
    residual_in,
    queries,
    key_cache,
    value_cache,
    lengths,
    out_weight,
    norm_gain,
    expert_ids,
    gate_values,
    w_gate,
    w_up,
    w_down,
):
    rows = queries.shape[0]
    head_dim = key_cache.shape[3]
    width = residual_in.shape[1]
    chips = lax.axis_size("dev")
    pieces = 8
    members = 4
    clusters = chips // members
    block = width // pieces

    teams = [[c * members + i for i in range(members)] for c in range(clusters)]
    core = lax.axis_index("role").astype(jnp.int32)
    half = out_weight.shape[0] // 2
    mine = lax.dynamic_slice_in_dim(out_weight, core * half, half, 0)
    mine = mine.reshape(half, members, width // members).transpose(1, 0, 2)
    mine = lax.all_to_all(mine, "dev", 0, 0, tiled=True, axis_index_groups=teams)
    other = lax.ppermute(mine, "role", [(0, 1), (1, 0)])

    context = attend(lengths, queries, key_cache, value_cache, clusters, members)
    context = context.reshape(chips, rows, members * head_dim)
    context = lax.all_to_all(context, "dev", 0, 0, tiled=True)
    part = project(core.reshape(1), context.reshape(chips * rows, members * head_dim), mine, other)
    part = lax.all_to_all(part.reshape(chips, rows, width // members), "dev", 0, 0, tiled=True)
    attn = jnp.sum(part.reshape(clusters, members, rows, width // members).astype(F32), axis=0)
    attn = attn.reshape(members, rows, pieces // members, block).transpose(0, 2, 1, 3)
    attn = attn.reshape(pieces, rows, block)

    residual = residual_in.reshape(rows, pieces, block).transpose(1, 0, 2)
    hidden = residual.astype(F32) + attn
    scale = lax.rsqrt(jnp.sum(hidden * hidden, axis=(0, 2), keepdims=True) / width + 1e-06)
    normed = (hidden * scale * norm_gain.reshape(pieces, 1, block)).astype(BF16)
    normed = normed.reshape(pieces * rows, block)

    top = expert_ids.shape[1]
    expert_total = chips * lax.axis_size("role")
    slots = 2
    pairs = rows * top
    flat = expert_ids.reshape(pairs)
    same = flat[:, None] == flat[None, :]
    before = jnp.arange(pairs)[:, None] > jnp.arange(pairs)[None, :]
    slot = jnp.sum((same & before).astype(jnp.int32), axis=1)
    target = (flat * slots + slot).reshape(rows, top)
    places = expert_total * slots * pieces
    spot = target[None] * pieces + jnp.arange(pieces, dtype=jnp.int32)[:, None, None]
    spot = spot.reshape(pieces * rows, top)
    chosen = jnp.zeros((places, pieces * rows), jnp.bool_)
    for k in range(top):
        chosen = chosen | (jnp.arange(places, dtype=jnp.int32)[:, None] == spot[:, k][None, :])
    outgoing = jnp.dot(chosen.astype(BF16), normed, preferred_element_type=F32).astype(BF16)
    arrived = lax.all_to_all(
        outgoing.reshape(expert_total, slots * pieces, block), ("role", "dev"), 0, 0, tiled=True
    )
    result = experts(
        arrived.reshape(places, block), w_gate[0], w_up[0], w_down[0], pieces
    )
    replies = lax.all_to_all(
        result.reshape(expert_total, slots * pieces, block), ("role", "dev"), 0, 0, tiled=True
    )
    mix = gate_values / jnp.sum(gate_values, axis=-1, keepdims=True)
    mix = jnp.broadcast_to(mix[None], (pieces, rows, top)).reshape(pieces * rows, top)
    mixer = jnp.zeros((pieces * rows, places), F32)
    for k in range(top):
        here = jnp.arange(places, dtype=jnp.int32)[None, :] == spot[:, k][:, None]
        mixer = mixer + jnp.where(here, mix[:, k][:, None], 0.0)
    rounded = lax.reduce_precision(mixer, exponent_bits=8, mantissa_bits=7)
    high = rounded.astype(BF16)
    low = (mixer - rounded).astype(BF16)
    both = jnp.dot(
        jnp.concatenate([high, low], axis=0),
        replies.reshape(places, block),
        preferred_element_type=F32,
    )
    mixed = hidden + (both[: pieces * rows] + both[pieces * rows :]).reshape(pieces, rows, block)
    return mixed.astype(BF16).transpose(1, 0, 2).reshape(rows, width)


def solution(mesh):
    both = ("role", "dev")
    return jax.shard_map(
        shards,
        mesh=mesh,
        in_specs=(
            P(both, None),
            P(both, None),
            P(both, None, None, None),
            P(both, None, None, None),
            P(both),
            P("dev", None),
            P(),
            P(both, None),
            P(both, None),
            P(both, None, None),
            P(both, None, None),
            P(both, None, None),
        ),
        out_specs=P(both, None),
        check_vma=False,
    )
```

```python
import functools
import math

import jax
import jax.numpy as jnp
import numpy as np
from jax import lax
from jax.experimental import pallas as pl
from jax.experimental.pallas import tpu as pltpu
from jax.sharding import PartitionSpec as P

BF16 = jnp.bfloat16
F32 = jnp.float32


def in_hbm(x):
    return pltpu.with_memory_space_constraint(x, pltpu.HBM)


def sign_table(order):
    signs = np.ones((1, 1), np.float32)
    while signs.shape[0] < order:
        signs = np.block([[signs, signs], [signs, -signs]])
    return signs


def attend_kernel(copies, len_ref, q_ref, k_ref, v_ref, table_ref, out_ref):
    rows, _, cache_len, dim = k_ref.shape
    heads = q_ref.shape[1] // dim
    total = rows * heads
    at = lax.broadcasted_iota(jnp.int32, (total, total), 0)
    to = lax.broadcasted_iota(jnp.int32, (total, total), 1)
    turn_in = (to == (at % heads) * rows + at // heads).astype(F32).astype(BF16)
    turn_out = (to == (at % rows) * heads + at // rows).astype(F32).astype(BF16)
    stacked = jnp.concatenate([q_ref[:, h * dim:(h + 1) * dim] for h in range(heads)], axis=0)
    q = jnp.dot(turn_in, stacked, preferred_element_type=F32).astype(BF16)
    position = lax.broadcasted_iota(jnp.int32, (heads, cache_len), 1)
    scores = []
    for r in range(rows):
        s = lax.dot_general(
            q[r * heads:(r + 1) * heads], k_ref[r, 0], (((1,), (1,)), ((), ())), preferred_element_type=F32
        )
        scores.append(jnp.where(position < len_ref[r], s * (1.0 / math.sqrt(dim)), -1e30))
    scores = jnp.concatenate(scores, axis=0)
    weights = jnp.exp(scores - jnp.max(scores, axis=-1, keepdims=True))
    probs = (weights / jnp.sum(weights, axis=-1, keepdims=True)).astype(BF16)
    rotated = jnp.concatenate(
        [
            jnp.dot(probs[r * heads:(r + 1) * heads], v_ref[r, 0], preferred_element_type=F32).astype(BF16)
            for r in range(rows)
        ],
        axis=0,
    )
    turned = jnp.dot(turn_out, rotated, preferred_element_type=F32).astype(BF16)
    context = jnp.dot(turned, table_ref[...], preferred_element_type=F32) * (1.0 / math.sqrt(dim))
    context = context.astype(BF16)
    each = out_ref.shape[3] // dim
    for h in range(heads):
        piece = context[h * rows:(h + 1) * rows]
        for c in range(copies):
            out_ref[h // each, c, :, (h % each) * dim:(h % each + 1) * dim] = piece


def attend(lengths, queries, key_cache, value_cache, clusters, copies):
    rows, kv_heads, cache_len, dim = key_cache.shape
    share = queries.shape[1] // kv_heads
    columns = queries.shape[1] // clusters
    table = jnp.asarray(sign_table(dim), BF16)
    per = clusters // kv_heads
    return pl.pallas_call(
        functools.partial(attend_kernel, copies),
        grid=(kv_heads,),
        out_shape=pltpu.HBM((clusters, copies, rows, columns), BF16),
        in_specs=[
            pl.BlockSpec(memory_space=pltpu.SMEM),
            pl.BlockSpec((rows, share), lambda i: (0, i)),
            pl.BlockSpec((rows, 1, cache_len, dim), lambda i: (0, i, 0, 0)),
            pl.BlockSpec((rows, 1, cache_len, dim), lambda i: (0, i, 0, 0)),
            pl.BlockSpec((dim, dim), lambda i: (0, 0)),
        ],
        out_specs=pl.BlockSpec((per, copies, rows, columns), lambda i: (i, 0, 0, 0)),
        compiler_params=pltpu.CompilerParams(vmem_limit_bytes=60 * 1024 * 1024),
        cost_estimate=pl.CostEstimate(
            flops=4 * rows * queries.shape[1] * cache_len,
            bytes_accessed=4 * rows * kv_heads * cache_len * dim + 2 * clusters * copies * rows * columns,
            transcendentals=rows * queries.shape[1] // dim * cache_len,
        ),
    )(lengths, queries, in_hbm(key_cache), in_hbm(value_cache), table)


WIDE, TALL, AHEAD = 384, 2048, 2


def expert_kernel(pieces, x_ref, gate_ref, up_hbm, down_hbm, out_hbm,
                  up_s, down_s, x_s, act_s, res_s, out_s, w_sem, d_sem, o_sem):
    group, block = x_ref.shape[1:]
    span = group // pieces
    parts, _, wide = up_s.shape
    outs, _, tall = down_s.shape
    loads = []
    for i in range(parts):
        cut = pl.ds(i * wide, wide)
        loads.append(pltpu.make_async_copy(up_hbm.at[:, cut], up_s.at[i], w_sem.at[i]))
    for i in range(outs):
        loads.append(pltpu.make_async_copy(down_hbm.at[:, pl.ds(i * tall, tall)], down_s.at[i], d_sem.at[i]))

    def arrive(n):
        loads[n].wait()
        if n + AHEAD < len(loads):
            loads[n + AHEAD].start()

    for first in loads[:AHEAD]:
        first.start()
    row = lax.broadcasted_iota(jnp.int32, (group, group), 0)
    col = lax.broadcasted_iota(jnp.int32, (group, group), 1)
    spread = (col == (row % span) * pieces + row // span).astype(F32).astype(BF16)
    gather = (row == (col % span) * pieces + col // span).astype(F32).astype(BF16)
    for g in range(x_ref.shape[0]):
        y = jnp.dot(spread, x_ref[g], preferred_element_type=F32).astype(BF16)
        for j in range(pieces):
            x_s[g * span:(g + 1) * span, j * block:(j + 1) * block] = y[j * span:(j + 1) * span, :]
    for i in range(parts):
        gate = jnp.dot(x_s[...], gate_ref[:, i * wide:(i + 1) * wide], preferred_element_type=F32)
        arrive(i)
        up = jnp.dot(x_s[...], up_s[i], preferred_element_type=F32)
        act_s[:, i * wide:(i + 1) * wide] = (gate / (1.0 + jnp.exp(-gate)) * up).astype(BF16)
    for i in range(outs):
        arrive(parts + i)
        y = jnp.dot(act_s[...], down_s[i], preferred_element_type=F32).astype(BF16)
        for n in range(tall // block):
            j = i * (tall // block) + n
            for g in range(x_ref.shape[0]):
                res_s[g, j * span:(j + 1) * span, :] = y[g * span:(g + 1) * span, n * block:(n + 1) * block]
    stores = []
    for g in range(x_ref.shape[0]):
        out_s[g] = jnp.dot(gather, res_s[g], preferred_element_type=F32).astype(BF16)
        store = pltpu.make_async_copy(out_s.at[g], out_hbm.at[g], o_sem.at[g])
        store.start()
        stores.append(store)
    for store in stores:
        store.wait()


def experts(x, w_gate, w_up, w_down, pieces):
    rows, block = x.shape
    width, hidden = w_gate.shape
    tokens = rows // pieces
    groups = pieces
    group = rows // groups
    wide, tall = min(WIDE, hidden), min(TALL, width)
    operands = [
        pltpu.with_memory_space_constraint(a, pltpu.VMEM)
        for a in (x.reshape(groups, group, block), w_gate)
    ] + [in_hbm(w_up), in_hbm(w_down)]
    result = pl.pallas_call(
        functools.partial(expert_kernel, pieces),
        out_shape=pltpu.HBM((groups, group, block), BF16),
        in_specs=[pl.BlockSpec(memory_space=pltpu.VMEM)] * 2 + [pl.BlockSpec(memory_space=pltpu.HBM)] * 2,
        out_specs=pl.BlockSpec(memory_space=pltpu.HBM),
        scratch_shapes=[
            pltpu.VMEM((hidden // wide, width, wide), BF16),
            pltpu.VMEM((width // tall, hidden, tall), BF16),
            pltpu.VMEM((tokens, width), BF16),
            pltpu.VMEM((tokens, hidden), BF16),
            pltpu.VMEM((groups, group, block), BF16),
            pltpu.VMEM((groups, group, block), BF16),
            pltpu.SemaphoreType.DMA((hidden // wide,)),
            pltpu.SemaphoreType.DMA((width // tall,)),
            pltpu.SemaphoreType.DMA((groups,)),
        ],
        compiler_params=pltpu.CompilerParams(vmem_limit_bytes=36 * 1024 * 1024),
        cost_estimate=pl.CostEstimate(
            flops=6 * tokens * width * hidden,
            bytes_accessed=4 * width * hidden + 4 * rows * block,
            transcendentals=tokens * hidden,
        ),
    )(*operands)
    return result.reshape(rows, block)


def project_kernel(me_ref, a_ref, mine_hbm, other_hbm, out_hbm, w_s, out_s, w_sem, o_sem):
    members, half, _ = mine_hbm.shape
    tiles, tile, _ = out_s.shape
    moves = []
    for n, source in enumerate((mine_hbm, other_hbm)):
        first = me_ref[0] if n == 0 else 1 - me_ref[0]
        for m in range(members):
            at = pl.multiple_of((2 * m + first) * half, half)
            moves.append(pltpu.make_async_copy(source.at[m], w_s.at[pl.ds(at, half)], w_sem.at[n, m]))
    for move in moves:
        move.start()
    for move in moves:
        move.wait()
    stores = []
    for t in range(tiles):
        out_s[t] = jnp.dot(
            a_ref[t * tile:(t + 1) * tile, :], w_s[...], preferred_element_type=F32
        ).astype(BF16)
        stores.append(pltpu.make_async_copy(out_s.at[t], out_hbm.at[t], o_sem.at[t]))
        stores[-1].start()
    for store in stores:
        store.wait()


def project(me, a, mine, other):
    rows, depth = a.shape
    members, half, columns = mine.shape
    tiles = 4
    result = pl.pallas_call(
        project_kernel,
        out_shape=pltpu.HBM((tiles, rows // tiles, columns), BF16),
        in_specs=[
            pl.BlockSpec(memory_space=pltpu.SMEM),
            pl.BlockSpec(memory_space=pltpu.VMEM),
            pl.BlockSpec(memory_space=pltpu.HBM),
            pl.BlockSpec(memory_space=pltpu.HBM),
        ],
        out_specs=pl.BlockSpec(memory_space=pltpu.HBM),
        scratch_shapes=[
            pltpu.VMEM((depth, columns), BF16),
            pltpu.VMEM((tiles, rows // tiles, columns), BF16),
            pltpu.SemaphoreType.DMA((2, members)),
            pltpu.SemaphoreType.DMA((tiles,)),
        ],
        compiler_params=pltpu.CompilerParams(vmem_limit_bytes=12 * 1024 * 1024),
        cost_estimate=pl.CostEstimate(
            flops=2 * rows * depth * columns,
            bytes_accessed=2 * (rows * depth + depth * columns + rows * columns),
            transcendentals=0,
        ),
    )(me, pltpu.with_memory_space_constraint(a, pltpu.VMEM), in_hbm(mine), in_hbm(other))
    return result.reshape(rows, columns)


def shards(
    residual_in,
    queries,
    key_cache,
    value_cache,
    lengths,
    out_weight,
    norm_gain,
    expert_ids,
    gate_values,
    w_gate,
    w_up,
    w_down,
):
    rows = queries.shape[0]
    head_dim = key_cache.shape[3]
    width = residual_in.shape[1]
    chips = lax.axis_size("dev")
    pieces = 8
    members = 4
    clusters = chips // members
    block = width // pieces

    teams = [[c * members + i for i in range(members)] for c in range(clusters)]
    core = lax.axis_index("role").astype(jnp.int32)
    half = out_weight.shape[0] // 2
    mine = lax.dynamic_slice_in_dim(out_weight, core * half, half, 0)
    mine = mine.reshape(half, members, width // members).transpose(1, 0, 2)
    mine = lax.all_to_all(mine, "dev", 0, 0, tiled=True, axis_index_groups=teams)
    other = lax.ppermute(mine, "role", [(0, 1), (1, 0)])

    context = attend(lengths, queries, key_cache, value_cache, clusters, members)
    context = context.reshape(chips, rows, members * head_dim)
    context = lax.all_to_all(context, "dev", 0, 0, tiled=True)
    part = project(core.reshape(1), context.reshape(chips * rows, members * head_dim), mine, other)
    part = lax.all_to_all(part.reshape(chips, rows, width // members), "dev", 0, 0, tiled=True)
    attn = jnp.sum(part.reshape(clusters, members, rows, width // members).astype(F32), axis=0)
    attn = attn.reshape(members, rows, pieces // members, block).transpose(0, 2, 1, 3)
    attn = attn.reshape(pieces, rows, block)

    residual = residual_in.reshape(rows, pieces, block).transpose(1, 0, 2)
    hidden = residual.astype(F32) + attn
    scale = lax.rsqrt(jnp.sum(hidden * hidden, axis=(0, 2), keepdims=True) / width + 1e-06)
    normed = (hidden * scale * norm_gain.reshape(pieces, 1, block)).astype(BF16)
    normed = normed.reshape(pieces * rows, block)

    top = expert_ids.shape[1]
    expert_total = chips * lax.axis_size("role")
    slots = 2
    pairs = rows * top
    flat = expert_ids.reshape(pairs)
    same = flat[:, None] == flat[None, :]
    before = jnp.arange(pairs)[:, None] > jnp.arange(pairs)[None, :]
    slot = jnp.sum((same & before).astype(jnp.int32), axis=1)
    target = (flat * slots + slot).reshape(rows, top)
    places = expert_total * slots * pieces
    spot = target[None] * pieces + jnp.arange(pieces, dtype=jnp.int32)[:, None, None]
    spot = spot.reshape(pieces * rows, top)
    chosen = jnp.zeros((places, pieces * rows), jnp.bool_)
    for k in range(top):
        chosen = chosen | (jnp.arange(places, dtype=jnp.int32)[:, None] == spot[:, k][None, :])
    outgoing = jnp.dot(chosen.astype(BF16), normed, preferred_element_type=F32).astype(BF16)
    arrived = lax.all_to_all(
        outgoing.reshape(expert_total, slots * pieces, block), ("role", "dev"), 0, 0, tiled=True
    )
    result = experts(
        arrived.reshape(places, block), w_gate[0], w_up[0], w_down[0], pieces
    )
    replies = lax.all_to_all(
        result.reshape(expert_total, slots * pieces, block), ("role", "dev"), 0, 0, tiled=True
    )
    mix = gate_values / jnp.sum(gate_values, axis=-1, keepdims=True)
    mix = jnp.broadcast_to(mix[None], (pieces, rows, top)).reshape(pieces * rows, top)
    mixer = jnp.zeros((pieces * rows, places), F32)
    for k in range(top):
        here = jnp.arange(places, dtype=jnp.int32)[None, :] == spot[:, k][:, None]
        mixer = mixer + jnp.where(here, mix[:, k][:, None], 0.0)
    rounded = lax.reduce_precision(mixer, exponent_bits=8, mantissa_bits=7)
    high = rounded.astype(BF16)
    low = (mixer - rounded).astype(BF16)
    both = jnp.dot(
        jnp.concatenate([high, low], axis=0),
        replies.reshape(places, block),
        preferred_element_type=F32,
    )
    mixed = hidden + (both[: pieces * rows] + both[pieces * rows :]).reshape(pieces, rows, block)
    return mixed.astype(BF16).transpose(1, 0, 2).reshape(rows, width)


def solution(mesh):
    both = ("role", "dev")
    return jax.shard_map(
        shards,
        mesh=mesh,
        in_specs=(
            P(both, None),
            P(both, None),
            P(both, None, None, None),
            P(both, None, None, None),
            P(both),
            P("dev", None),
            P(),
            P(both, None),
            P(both, None),
            P(both, None, None),
            P(both, None, None),
            P(both, None, None),
        ),
        out_specs=P(both, None),
        check_vma=False,
    )
```

```python
import functools
import math

import jax
import jax.numpy as jnp
import numpy as np
from jax import lax
from jax.experimental import pallas as pl
from jax.experimental.pallas import tpu as pltpu
from jax.sharding import PartitionSpec as P

BF16 = jnp.bfloat16
F32 = jnp.float32


def in_hbm(x):
    return pltpu.with_memory_space_constraint(x, pltpu.HBM)


def sign_table(order):
    signs = np.ones((1, 1), np.float32)
    while signs.shape[0] < order:
        signs = np.block([[signs, signs], [signs, -signs]])
    return signs


def attend_kernel(copies, len_ref, q_ref, k_ref, v_ref, table_ref, out_ref):
    rows, _, cache_len, dim = k_ref.shape
    heads = q_ref.shape[1] // dim
    total = rows * heads
    at = lax.broadcasted_iota(jnp.int32, (total, total), 0)
    to = lax.broadcasted_iota(jnp.int32, (total, total), 1)
    turn_in = (to == (at % heads) * rows + at // heads).astype(F32).astype(BF16)
    turn_out = (to == (at % rows) * heads + at // rows).astype(F32).astype(BF16)
    stacked = jnp.concatenate([q_ref[:, h * dim:(h + 1) * dim] for h in range(heads)], axis=0)
    q = jnp.dot(turn_in, stacked, preferred_element_type=F32).astype(BF16)
    position = lax.broadcasted_iota(jnp.int32, (heads, cache_len), 1)
    scores = []
    for r in range(rows):
        s = lax.dot_general(
            q[r * heads:(r + 1) * heads], k_ref[r, 0], (((1,), (1,)), ((), ())), preferred_element_type=F32
        )
        scores.append(jnp.where(position < len_ref[r], s * (1.0 / math.sqrt(dim)), -1e30))
    scores = jnp.concatenate(scores, axis=0)
    weights = jnp.exp(scores - jnp.max(scores, axis=-1, keepdims=True))
    probs = (weights / jnp.sum(weights, axis=-1, keepdims=True)).astype(BF16)
    rotated = jnp.concatenate(
        [
            jnp.dot(probs[r * heads:(r + 1) * heads], v_ref[r, 0], preferred_element_type=F32).astype(BF16)
            for r in range(rows)
        ],
        axis=0,
    )
    turned = jnp.dot(turn_out, rotated, preferred_element_type=F32).astype(BF16)
    context = jnp.dot(turned, table_ref[...], preferred_element_type=F32) * (1.0 / math.sqrt(dim))
    context = context.astype(BF16)
    each = out_ref.shape[3] // dim
    for h in range(heads):
        piece = context[h * rows:(h + 1) * rows]
        for c in range(copies):
            out_ref[h // each, c, :, (h % each) * dim:(h % each + 1) * dim] = piece


def attend(lengths, queries, key_cache, value_cache, clusters, copies):
    rows, kv_heads, cache_len, dim = key_cache.shape
    share = queries.shape[1] // kv_heads
    columns = queries.shape[1] // clusters
    table = jnp.asarray(sign_table(dim), BF16)
    per = clusters // kv_heads
    return pl.pallas_call(
        functools.partial(attend_kernel, copies),
        grid=(kv_heads,),
        out_shape=pltpu.HBM((clusters, copies, rows, columns), BF16),
        in_specs=[
            pl.BlockSpec(memory_space=pltpu.SMEM),
            pl.BlockSpec((rows, share), lambda i: (0, i)),
            pl.BlockSpec((rows, 1, cache_len, dim), lambda i: (0, i, 0, 0)),
            pl.BlockSpec((rows, 1, cache_len, dim), lambda i: (0, i, 0, 0)),
            pl.BlockSpec((dim, dim), lambda i: (0, 0)),
        ],
        out_specs=pl.BlockSpec((per, copies, rows, columns), lambda i: (i, 0, 0, 0)),
        compiler_params=pltpu.CompilerParams(vmem_limit_bytes=60 * 1024 * 1024),
        cost_estimate=pl.CostEstimate(
            flops=4 * rows * queries.shape[1] * cache_len,
            bytes_accessed=4 * rows * kv_heads * cache_len * dim + 2 * clusters * copies * rows * columns,
            transcendentals=rows * queries.shape[1] // dim * cache_len,
        ),
    )(lengths, queries, in_hbm(key_cache), in_hbm(value_cache), table)


WIDE, TALL, AHEAD = 384, 1024, 3


def expert_kernel(pieces, x_ref, gate_ref, up_hbm, down_hbm, out_hbm,
                  up_s, down_s, x_s, act_s, res_s, out_s, w_sem, d_sem, o_sem):
    group, block = x_ref.shape[1:]
    span = group // pieces
    parts, _, wide = up_s.shape
    outs, _, tall = down_s.shape
    loads = []
    for i in range(parts):
        cut = pl.ds(i * wide, wide)
        loads.append(pltpu.make_async_copy(up_hbm.at[:, cut], up_s.at[i], w_sem.at[i]))
    for i in range(outs):
        loads.append(pltpu.make_async_copy(down_hbm.at[:, pl.ds(i * tall, tall)], down_s.at[i], d_sem.at[i]))

    def arrive(n):
        loads[n].wait()
        if n + AHEAD < len(loads):
            loads[n + AHEAD].start()

    for first in loads[:AHEAD]:
        first.start()
    row = lax.broadcasted_iota(jnp.int32, (group, group), 0)
    col = lax.broadcasted_iota(jnp.int32, (group, group), 1)
    spread = (col == (row % span) * pieces + row // span).astype(F32).astype(BF16)
    gather = (row == (col % span) * pieces + col // span).astype(F32).astype(BF16)
    for g in range(x_ref.shape[0]):
        y = jnp.dot(spread, x_ref[g], preferred_element_type=F32).astype(BF16)
        for j in range(pieces):
            x_s[g * span:(g + 1) * span, j * block:(j + 1) * block] = y[j * span:(j + 1) * span, :]
    for i in range(parts):
        gate = jnp.dot(x_s[...], gate_ref[:, i * wide:(i + 1) * wide], preferred_element_type=F32)
        arrive(i)
        up = jnp.dot(x_s[...], up_s[i], preferred_element_type=F32)
        act_s[:, i * wide:(i + 1) * wide] = (gate / (1.0 + jnp.exp(-gate)) * up).astype(BF16)
    for i in range(outs):
        arrive(parts + i)
        y = jnp.dot(act_s[...], down_s[i], preferred_element_type=F32).astype(BF16)
        for n in range(tall // block):
            j = i * (tall // block) + n
            for g in range(x_ref.shape[0]):
                res_s[g, j * span:(j + 1) * span, :] = y[g * span:(g + 1) * span, n * block:(n + 1) * block]
    stores = []
    for g in range(x_ref.shape[0]):
        out_s[g] = jnp.dot(gather, res_s[g], preferred_element_type=F32).astype(BF16)
        store = pltpu.make_async_copy(out_s.at[g], out_hbm.at[g], o_sem.at[g])
        store.start()
        stores.append(store)
    for store in stores:
        store.wait()


def experts(x, w_gate, w_up, w_down, pieces):
    rows, block = x.shape
    width, hidden = w_gate.shape
    tokens = rows // pieces
    groups = pieces
    group = rows // groups
    wide, tall = min(WIDE, hidden), min(TALL, width)
    operands = [
        pltpu.with_memory_space_constraint(a, pltpu.VMEM)
        for a in (x.reshape(groups, group, block), w_gate)
    ] + [in_hbm(w_up), in_hbm(w_down)]
    result = pl.pallas_call(
        functools.partial(expert_kernel, pieces),
        out_shape=pltpu.HBM((groups, group, block), BF16),
        in_specs=[pl.BlockSpec(memory_space=pltpu.VMEM)] * 2 + [pl.BlockSpec(memory_space=pltpu.HBM)] * 2,
        out_specs=pl.BlockSpec(memory_space=pltpu.HBM),
        scratch_shapes=[
            pltpu.VMEM((hidden // wide, width, wide), BF16),
            pltpu.VMEM((width // tall, hidden, tall), BF16),
            pltpu.VMEM((tokens, width), BF16),
            pltpu.VMEM((tokens, hidden), BF16),
            pltpu.VMEM((groups, group, block), BF16),
            pltpu.VMEM((groups, group, block), BF16),
            pltpu.SemaphoreType.DMA((hidden // wide,)),
            pltpu.SemaphoreType.DMA((width // tall,)),
            pltpu.SemaphoreType.DMA((groups,)),
        ],
        compiler_params=pltpu.CompilerParams(vmem_limit_bytes=36 * 1024 * 1024),
        cost_estimate=pl.CostEstimate(
            flops=6 * tokens * width * hidden,
            bytes_accessed=4 * width * hidden + 4 * rows * block,
            transcendentals=tokens * hidden,
        ),
    )(*operands)
    return result.reshape(rows, block)


def project_kernel(me_ref, a_ref, mine_hbm, other_hbm, out_hbm, w_s, out_s, w_sem, o_sem):
    members, half, _ = mine_hbm.shape
    tiles, tile, _ = out_s.shape
    moves = []
    for n, source in enumerate((mine_hbm, other_hbm)):
        first = me_ref[0] if n == 0 else 1 - me_ref[0]
        for m in range(members):
            at = pl.multiple_of((2 * m + first) * half, half)
            moves.append(pltpu.make_async_copy(source.at[m], w_s.at[pl.ds(at, half)], w_sem.at[n, m]))
    for move in moves:
        move.start()
    for move in moves:
        move.wait()
    stores = []
    for t in range(tiles):
        out_s[t] = jnp.dot(
            a_ref[t * tile:(t + 1) * tile, :], w_s[...], preferred_element_type=F32
        ).astype(BF16)
        stores.append(pltpu.make_async_copy(out_s.at[t], out_hbm.at[t], o_sem.at[t]))
        stores[-1].start()
    for store in stores:
        store.wait()


def project(me, a, mine, other):
    rows, depth = a.shape
    members, half, columns = mine.shape
    tiles = 8
    result = pl.pallas_call(
        project_kernel,
        out_shape=pltpu.HBM((tiles, rows // tiles, columns), BF16),
        in_specs=[
            pl.BlockSpec(memory_space=pltpu.SMEM),
            pl.BlockSpec(memory_space=pltpu.VMEM),
            pl.BlockSpec(memory_space=pltpu.HBM),
            pl.BlockSpec(memory_space=pltpu.HBM),
        ],
        out_specs=pl.BlockSpec(memory_space=pltpu.HBM),
        scratch_shapes=[
            pltpu.VMEM((depth, columns), BF16),
            pltpu.VMEM((tiles, rows // tiles, columns), BF16),
            pltpu.SemaphoreType.DMA((2, members)),
            pltpu.SemaphoreType.DMA((tiles,)),
        ],
        compiler_params=pltpu.CompilerParams(vmem_limit_bytes=12 * 1024 * 1024),
        cost_estimate=pl.CostEstimate(
            flops=2 * rows * depth * columns,
            bytes_accessed=2 * (rows * depth + depth * columns + rows * columns),
            transcendentals=0,
        ),
    )(me, pltpu.with_memory_space_constraint(a, pltpu.VMEM), in_hbm(mine), in_hbm(other))
    return result.reshape(rows, columns)


def shards(
    residual_in,
    queries,
    key_cache,
    value_cache,
    lengths,
    out_weight,
    norm_gain,
    expert_ids,
    gate_values,
    w_gate,
    w_up,
    w_down,
):
    rows = queries.shape[0]
    head_dim = key_cache.shape[3]
    width = residual_in.shape[1]
    chips = lax.axis_size("dev")
    pieces = 8
    members = 4
    clusters = chips // members
    block = width // pieces

    teams = [[c * members + i for i in range(members)] for c in range(clusters)]
    core = lax.axis_index("role").astype(jnp.int32)
    half = out_weight.shape[0] // 2
    mine = lax.dynamic_slice_in_dim(out_weight, core * half, half, 0)
    mine = mine.reshape(half, members, width // members).transpose(1, 0, 2)
    mine = lax.all_to_all(mine, "dev", 0, 0, tiled=True, axis_index_groups=teams)
    other = lax.ppermute(mine, "role", [(0, 1), (1, 0)])

    context = attend(lengths, queries, key_cache, value_cache, clusters, members)
    context = context.reshape(chips, rows, members * head_dim)
    context = lax.all_to_all(context, "dev", 0, 0, tiled=True)
    part = project(core.reshape(1), context.reshape(chips * rows, members * head_dim), mine, other)
    part = lax.all_to_all(part.reshape(chips, rows, width // members), "dev", 0, 0, tiled=True)
    attn = jnp.sum(part.reshape(clusters, members, rows, width // members).astype(F32), axis=0)
    attn = attn.reshape(members, rows, pieces // members, block).transpose(0, 2, 1, 3)
    attn = attn.reshape(pieces, rows, block)

    residual = residual_in.reshape(rows, pieces, block).transpose(1, 0, 2)
    hidden = residual.astype(F32) + attn
    scale = lax.rsqrt(jnp.sum(hidden * hidden, axis=(0, 2), keepdims=True) / width + 1e-06)
    normed = (hidden * scale * norm_gain.reshape(pieces, 1, block)).astype(BF16)
    normed = normed.reshape(pieces * rows, block)

    top = expert_ids.shape[1]
    expert_total = chips * lax.axis_size("role")
    slots = 2
    pairs = rows * top
    flat = expert_ids.reshape(pairs)
    same = flat[:, None] == flat[None, :]
    before = jnp.arange(pairs)[:, None] > jnp.arange(pairs)[None, :]
    slot = jnp.sum((same & before).astype(jnp.int32), axis=1)
    target = (flat * slots + slot).reshape(rows, top)
    places = expert_total * slots * pieces
    spot = target[None] * pieces + jnp.arange(pieces, dtype=jnp.int32)[:, None, None]
    spot = spot.reshape(pieces * rows, top)
    chosen = jnp.zeros((places, pieces * rows), jnp.bool_)
    for k in range(top):
        chosen = chosen | (jnp.arange(places, dtype=jnp.int32)[:, None] == spot[:, k][None, :])
    outgoing = jnp.dot(chosen.astype(BF16), normed, preferred_element_type=F32).astype(BF16)
    arrived = lax.all_to_all(
        outgoing.reshape(expert_total, slots * pieces, block), ("role", "dev"), 0, 0, tiled=True
    )
    result = experts(
        arrived.reshape(places, block), w_gate[0], w_up[0], w_down[0], pieces
    )
    replies = lax.all_to_all(
        result.reshape(expert_total, slots * pieces, block), ("role", "dev"), 0, 0, tiled=True
    )
    mix = gate_values / jnp.sum(gate_values, axis=-1, keepdims=True)
    mix = jnp.broadcast_to(mix[None], (pieces, rows, top)).reshape(pieces * rows, top)
    mixer = jnp.zeros((pieces * rows, places), F32)
    for k in range(top):
        here = jnp.arange(places, dtype=jnp.int32)[None, :] == spot[:, k][:, None]
        mixer = mixer + jnp.where(here, mix[:, k][:, None], 0.0)
    rounded = lax.reduce_precision(mixer, exponent_bits=8, mantissa_bits=7)
    high = rounded.astype(BF16)
    low = (mixer - rounded).astype(BF16)
    both = jnp.dot(
        jnp.concatenate([high, low], axis=0),
        replies.reshape(places, block),
        preferred_element_type=F32,
    )
    mixed = hidden + (both[: pieces * rows] + both[pieces * rows :]).reshape(pieces, rows, block)
    return mixed.astype(BF16).transpose(1, 0, 2).reshape(rows, width)


def solution(mesh):
    both = ("role", "dev")
    return jax.shard_map(
        shards,
        mesh=mesh,
        in_specs=(
            P(both, None),
            P(both, None),
            P(both, None, None, None),
            P(both, None, None, None),
            P(both),
            P("dev", None),
            P(),
            P(both, None),
            P(both, None),
            P(both, None, None),
            P(both, None, None),
            P(both, None, None),
        ),
        out_specs=P(both, None),
        check_vma=False,
    )
```
